32 devices in a mesh: basis: 8 (over y, x, core), orb: 4 (over z).
Axes of the slice: x: 2, y: 2, z: 4, core: 2. Of those that a mesh axis runs over, the one named last changes fastest.
Arguments:
- cont_orbitals: bfloat16 [32768, 2048], P('basis', 'orb'), may hold values from -6 to 6
- target_orbitals: bfloat16 [32768, 1024], P('basis'), may hold values from -0.09375 to 0.09375
- margin_blocks: bfloat16 [128, 4, 256, 256], P('basis'), may hold values from -0.1875 to 0.1875
- dipole_blocks: bfloat16 [128, 4, 256, 256], P('basis'), may hold values from -0.1875 to 0.1875
- band_offsets: int32 [128, 4], P('basis'), may hold values from -2 to 2, as said below
Outputs:
- cont_orth: bfloat16 [32768, 2048], P('basis', 'orb')
- dipole_mo: bfloat16 [1024, 2048], P('basis', 'orb')
The draws below stay inside these ranges and needn't reach their ends.
Inputs may be any that keep to these rules, and one draw needn't show every extreme that they name: `band_offsets`: each block row names 4 different offsets.
All inputs are finite; a program needn't handle non-finite values.
Results may differ from the reference program's by a relative error of at most 0.012.
Values may be sent and summed in bfloat16 or wider, within the bound.
No kernel may reach another device: no remote copies, remote signals or barrier semaphores. Data moves between devices by JAX's collectives and lax.ppermute only.
A program may use at most 128 MiB of HBM per device.

```python
import jax
import jax.numpy as jnp
from jax import lax

BK = 256
KB = 4
NT = 1024
NC = 2048
NBLK = 128
NB = 32768


def draw_band_offsets(key, part):
    dropped = jax.random.randint(key, (NBLK, 1), 0, 5)
    base = jnp.arange(4, dtype=jnp.int32)[None, :]
    shifted = base + (base >= dropped).astype(jnp.int32) - 2
    return shifted.astype(jnp.int32)


def block_scale(key, shape, cuts, least, high):
    loudness = 1.0
    for dim, parts in cuts:
        draws = jax.random.uniform(jax.random.fold_in(jax.random.fold_in(key, 6), dim), (parts,), jnp.float32, least / len(cuts), high / len(cuts))
        loudness = loudness * jnp.repeat(jnp.exp(draws), shape[dim] // parts).reshape((-1,) + (1,) * (len(shape) - 1 - dim))
    return loudness


def noise(key, extent, scale, most, pieces=(), held_as=jnp.bfloat16):
    entries = jax.random.normal(key, extent, jnp.float32) * scale
    if len(pieces) > 0:
        entries = block_scale(key, extent, pieces, -0.22, 0.18) * entries
    return jnp.clip(entries, min=-most, max=most).astype(held_as)


def setup_inputs(seed: int = 0) -> dict:
    seeds = jax.random.split(jax.random.key(seed), 6)
    return {
        "cont_orbitals": noise(seeds[0], (NB, NC), 1.0, 6.0, ((0, 8), (1, 4))),
        "target_orbitals": noise(seeds[1], (NB, NT), (4 * NT) ** -0.5, 0.09375, ((0, 8),)),
        "margin_blocks": noise(seeds[2], (NBLK, KB, BK, BK), (KB * BK) ** -0.5, 0.1875, ((0, 8),)),
        "dipole_blocks": noise(seeds[3], (NBLK, KB, BK, BK), (KB * BK) ** -0.5, 0.1875, ((0, 8),)),
        "band_offsets": draw_band_offsets(jax.random.fold_in(seeds[5], 71), 0),
    }


def band_apply(blocks, offsets, field):
    nblk = blocks.shape[0]
    width = field.shape[1]
    padded = jnp.pad(field, ((2 * BK, 2 * BK), (0, 0))).reshape(nblk + 4, BK, width)
    total = jnp.zeros((nblk, BK, width), jnp.float32)
    for k in range(KB):
        index = (jnp.arange(nblk, dtype=jnp.int32) + 2 + offsets[:, k].astype(jnp.int32)).astype(jnp.int32)
        taken = padded[index]
        total = total + jnp.einsum('bij,bjc->bic', blocks[:, k].astype(jnp.float32), taken.astype(jnp.float32))
    return total.reshape(nblk * BK, width)

def reference(cont_orbitals, target_orbitals, margin_blocks, dipole_blocks, band_offsets):
    margin_cont = band_apply(margin_blocks, band_offsets, cont_orbitals).astype(jnp.bfloat16)
    projection = jnp.dot(target_orbitals.T, margin_cont, preferred_element_type=jnp.float32)
    projection_b = projection.astype(jnp.bfloat16)
    removed = jnp.dot(target_orbitals, projection_b, preferred_element_type=jnp.float32)
    cont_orth = (cont_orbitals.astype(jnp.float32) - removed).astype(jnp.bfloat16)
    squares = lax.optimization_barrier(jnp.sum(jnp.square(cont_orth.astype(jnp.float32)), axis=0))
    col_norm = 1.0 / jnp.sqrt(squares / NB + 1e-06)
    dipole_cont = band_apply(dipole_blocks, band_offsets, cont_orth).astype(jnp.bfloat16)
    dipole_raw = jnp.dot(target_orbitals.T, dipole_cont, preferred_element_type=jnp.float32)
    dipole_mo = (dipole_raw * col_norm[None, :]).astype(jnp.bfloat16)
    return (cont_orth, dipole_mo)
```

```python
import functools

import jax
import jax.numpy as jnp
from jax import lax
from jax.experimental import pallas as pl
from jax.experimental.pallas import tpu as pltpu
from jax.sharding import PartitionSpec as P

BK = 256
KB = 4
PAD = 16
F32 = jnp.float32
BF16 = jnp.bfloat16
ANY = pl.BlockSpec(memory_space=pl.ANY)
VMEM = pl.BlockSpec(memory_space=pltpu.VMEM)
SMEM = pl.BlockSpec(memory_space=pltpu.SMEM)


def params(mib=40):
    return pltpu.CompilerParams(vmem_limit_bytes=mib * 2**20)


def cost(macs, data):
    return pl.CostEstimate(flops=2 * macs, bytes_accessed=data, transcendentals=0)


def dot(a, b, dims=((1,), (0,))):
    return lax.dot_general(a, b, (dims, ((), ())), preferred_element_type=F32)


class Loads:
    def __init__(self, sems):
        self.sems, self.copies, self.done = sems, [], set()

    def start(self, src, dst):
        copy = pltpu.make_async_copy(src, dst, self.sems.at[len(self.copies)])
        copy.start()
        self.copies.append(copy)
        return len(self.copies) - 1

    def wait(self, *which):
        for i in which:
            if i not in self.done:
                self.copies[i].wait()
                self.done.add(i)


def band_rows(rows, slots, off, field, blocks, base, ys):
    for r, (b, slot) in enumerate(zip(rows, slots)):
        total = None
        for k in range(KB):
            term = dot(blocks[slot, k], field[b + off[k, b] + base])
            total = term if total is None else total + term
        ys[r * BK : (r + 1) * BK, :] = total.astype(BF16)


def groups_of(nblk):
    inner = list(range(2, nblk - 2))
    return [inner[i : i + 4] for i in range(0, len(inner), 4)]


def interior_kernel(nblk, off, c, t, m, out, c_v, t_v, m_v, ys, sems):
    loads = Loads(sems)
    have, needs = 0, []
    for rows in groups_of(nblk):
        lo, hi = rows[0], rows[-1] + 1
        mid = min(lo + 2, hi)
        want = []
        for part in ((lo, mid), (mid, hi)):
            if part[0] == part[1]:
                continue
            upto = part[1] + 2
            ids = []
            if upto > have:
                ids.append(loads.start(c.at[have:upto], c_v.at[have:upto]))
                have = upto
            ids.append(
                loads.start(m.at[part[0] : part[1]], m_v.at[part[0] - 2 : part[1] - 2])
            )
            want.append((list(range(*part)), ids))
        t_id = loads.start(t.at[lo:hi], t_v.at[lo - 2 : hi - 2])
        needs.append((rows, want, t_id))
    for g, (rows, want, t_id) in enumerate(needs):
        at = 0
        for part, ids in want:
            loads.wait(*ids)
            band_rows(
                part, [b - 2 for b in part], off, c_v, m_v, 0,
                ys.at[at * BK : (at + len(part)) * BK],
            )
            at += len(part)
        loads.wait(t_id)
        lo, size = rows[0] - 2, len(rows) * BK
        piece = dot(ys[0:size, :], t_v[lo : lo + len(rows)].reshape(size, -1), ((0,), (0,)))
        if g == 0:
            out[...] = piece
        else:
            out[...] += piece


def project_interior(off, c, t, m):
    nblk, _, w = c.shape
    nt = t.shape[2]
    inner = nblk - 4
    return pl.pallas_call(
        functools.partial(interior_kernel, nblk),
        out_shape=jax.ShapeDtypeStruct((w, nt), F32),
        in_specs=[SMEM, ANY, ANY, ANY],
        out_specs=VMEM,
        scratch_shapes=[
            pltpu.VMEM((nblk, BK, w), BF16),
            pltpu.VMEM((inner, BK, nt), BF16),
            pltpu.VMEM((inner, KB, BK, BK), BF16),
            pltpu.VMEM((4 * BK, w), BF16),
            pltpu.SemaphoreType.DMA((5 * len(groups_of(nblk)),)),
        ],
        compiler_params=params(),
        cost_estimate=cost(inner * BK * w * (KB * BK + nt), 2 * (c.size + t.size + m.size)),
    )(off, c, t, m)


def boundary_rows(nblk, core, off, f, intra, inter, t, m, f_v, t_v, m_v, ys, sems):
    loads = Loads(sems)
    parts = []
    for side, at, home in ((0, 0, 2), (1, nblk - 2, 6)):
        ids = [loads.start(m.at[at : at + 2], m_v.at[2 * side : 2 * side + 2])]
        near = 0 if side == 0 else nblk - 4
        ids.append(loads.start(f.at[near : near + 4], f_v.at[home : home + 4]))
        parts.append(ids)
    low = 10 * (1 - core)
    parts[0].append(loads.start(intra, f_v.at[pl.ds(low, 2)]))
    parts[0].append(loads.start(inter, f_v.at[pl.ds(10 - low, 2)]))
    for side, at in ((0, 0), (1, nblk - 2)):
        parts[1].append(loads.start(t.at[at : at + 2], t_v.at[2 * side : 2 * side + 2]))
    loads.wait(*parts[0])
    band_rows([0, 1], [0, 1], off, f_v, m_v, 2, ys.at[0 : 2 * BK])
    loads.wait(*parts[1])
    band_rows(
        [nblk - 2, nblk - 1], [2, 3], off, f_v, m_v, 10 - nblk, ys.at[2 * BK : 4 * BK]
    )
    return dot(ys[...], t_v[...].reshape(4 * BK, -1), ((0,), (0,)))


def boundary_scratch(w, nt):
    return [
        pltpu.VMEM((12, BK, w), BF16),
        pltpu.VMEM((4, BK, nt), BF16),
        pltpu.VMEM((4, KB, BK, BK), BF16),
        pltpu.VMEM((4 * BK, w), BF16),
        pltpu.SemaphoreType.DMA((8,)),
    ]


def boundary_kernel(nblk, core, off, acc, c, intra, inter, t, m, send, keep, total, *scratch):
    half = send.shape[0]
    total[...] = acc[...] + boundary_rows(
        nblk, core[0], off, c, intra, inter, t, m, *scratch
    )
    here = pl.multiple_of(core[0] * half, half)
    there = pl.multiple_of((1 - core[0]) * half, half)
    send[...] = total[pl.ds(there, half), :].astype(BF16)
    keep[...] = total[pl.ds(here, half), :]


def project_boundary(core, off, acc, c, intra, inter, t, m):
    nblk, _, w = c.shape
    nt = t.shape[2]
    return pl.pallas_call(
        functools.partial(boundary_kernel, nblk),
        out_shape=(
            jax.ShapeDtypeStruct((w // 2, nt), BF16),
            jax.ShapeDtypeStruct((w // 2, nt), F32),
        ),
        in_specs=[SMEM, SMEM, VMEM, ANY, ANY, ANY, ANY, ANY],
        out_specs=(VMEM, VMEM),
        scratch_shapes=[pltpu.VMEM((w, nt), F32)] + boundary_scratch(w, nt),
        compiler_params=params(),
        cost_estimate=cost(4 * BK * w * (KB * BK + nt), 8 * 2**20),
    )(core, off, acc, c, intra, inter, t, m)


def orth_rows(c, t, p):
    return (c.astype(F32) - dot(t, p, ((1,), (1,)))).astype(BF16)


def place_projection(core, mine, other, p):
    half = mine.shape[0]
    p[pl.ds(pl.multiple_of(core * half, half), half), :] = mine[...]
    p[pl.ds(pl.multiple_of((1 - core) * half, half), half), :] = other[...]


def square_sum(x):
    x = x.astype(F32)
    return jnp.sum(x * x, axis=0, keepdims=True)


def edge_kernel(nblk, core, mine, other, c, t, edge, intra, inter, sq, c_v, t_v, p, sems):
    loads = Loads(sems)
    ids = []
    for side, at in ((0, 0), (1, nblk - 2)):
        ids.append(
            (
                loads.start(c.at[at : at + 2], c_v.at[2 * side : 2 * side + 2]),
                loads.start(t.at[at : at + 2], t_v.at[2 * side : 2 * side + 2]),
            )
        )
    place_projection(core[0], mine, other, p)
    sq[...] = jnp.zeros_like(sq)
    for side in range(2):
        loads.wait(*ids[side])
        for r in range(2):
            i = 2 * side + r
            x = orth_rows(c_v[i], t_v[i], p[...])
            edge[i] = x
            sq[...] += square_sum(x)

            @pl.when(core[0] == side)
            def _(x=x, r=r):
                inter[r] = x

            @pl.when(core[0] != side)
            def _(x=x, r=r):
                intra[r] = x


def orth_edges(core, mine, other, c, t):
    nblk, _, w = c.shape
    nt = t.shape[2]
    pair = jax.ShapeDtypeStruct((2, BK, w), BF16)
    return pl.pallas_call(
        functools.partial(edge_kernel, nblk),
        out_shape=(
            jax.ShapeDtypeStruct((4, BK, w), BF16),
            pair,
            pair,
            jax.ShapeDtypeStruct((1, w), F32),
        ),
        in_specs=[SMEM, VMEM, VMEM, ANY, ANY],
        out_specs=(VMEM,) * 4,
        scratch_shapes=[
            pltpu.VMEM((4, BK, w), BF16),
            pltpu.VMEM((4, BK, nt), BF16),
            pltpu.VMEM((w, nt), BF16),
            pltpu.SemaphoreType.DMA((4,)),
        ],
        compiler_params=params(),
        cost_estimate=cost(4 * BK * w * nt, 4 * 2**20),
    )(core, mine, other, c, t)


def orth_dipole_kernel(
    nblk, core, off, mine, other, c, t, d, edge, sq_in, x_out, out, sq,
    c_v, t_v, d_v, x_v, ys, p, sems, out_sems,
):
    loads = Loads(sems)
    groups = groups_of(nblk)
    low = loads.start(edge.at[0:2], x_v.at[0:2])
    high = loads.start(edge.at[2:4], x_v.at[nblk - 2 : nblk])
    ct_ids, d_ids = [], []
    for rows in groups:
        lo, hi = rows[0], rows[-1] + 1
        ct_ids.append(
            (
                loads.start(c.at[lo:hi], c_v.at[lo - 2 : hi - 2]),
                loads.start(t.at[lo:hi], t_v.at[lo - 2 : hi - 2]),
            )
        )
    for rows in groups:
        lo, hi = rows[0], rows[-1] + 1
        d_ids.append(loads.start(d.at[lo:hi], d_v.at[lo - 2 : hi - 2]))
    place_projection(core[0], mine, other, p)
    sq[...] = sq_in[...]
    stores = Loads(out_sems)
    for rows, ids in zip(groups, ct_ids):
        loads.wait(*ids)
        for b in rows:
            x = orth_rows(c_v[b - 2], t_v[b - 2], p[...])
            x_v[b] = x
            sq[...] += square_sum(x)
        stores.start(
            x_v.at[rows[0] : rows[-1] + 1], x_out.at[rows[0] : rows[-1] + 1]
        )
    loads.wait(low, high)
    stores.start(x_v.at[0:2], x_out.at[0:2])
    stores.start(x_v.at[nblk - 2 : nblk], x_out.at[nblk - 2 : nblk])
    for g, (rows, d_id) in enumerate(zip(groups, d_ids)):
        loads.wait(d_id)
        lo, size = rows[0] - 2, len(rows) * BK
        band_rows(rows, [b - 2 for b in rows], off, x_v, d_v, 0, ys.at[0:size])
        piece = dot(ys[0:size, :], t_v[lo : lo + len(rows)].reshape(size, -1), ((0,), (0,)))
        if g == 0:
            out[...] = piece
        else:
            out[...] += piece
    stores.wait(*range(len(stores.copies)))


def orth_dipole_interior(core, off, mine, other, c, t, d, edge, sq):
    nblk, _, w = c.shape
    nt = t.shape[2]
    inner = nblk - 4
    count = len(groups_of(nblk))
    return pl.pallas_call(
        functools.partial(orth_dipole_kernel, nblk),
        out_shape=(
            jax.ShapeDtypeStruct((nblk, BK, w), BF16),
            jax.ShapeDtypeStruct((w, nt), F32),
            jax.ShapeDtypeStruct((1, w), F32),
        ),
        in_specs=[SMEM, SMEM, VMEM, VMEM, ANY, ANY, ANY, ANY, VMEM],
        out_specs=(ANY, VMEM, VMEM),
        scratch_shapes=[
            pltpu.VMEM((inner, BK, w), BF16),
            pltpu.VMEM((inner, BK, nt), BF16),
            pltpu.VMEM((inner, KB, BK, BK), BF16),
            pltpu.VMEM((nblk, BK, w), BF16),
            pltpu.VMEM((4 * BK, w), BF16),
            pltpu.VMEM((w, nt), BF16),
            pltpu.SemaphoreType.DMA((2 + 3 * count,)),
            pltpu.SemaphoreType.DMA((2 + count,)),
        ],
        compiler_params=params(),
        cost_estimate=cost(inner * BK * w * (KB * BK + 2 * nt), 24 * 2**20),
    )(core, off, mine, other, c, t, d, edge, sq)


def put_squares(msg, g, sq, w):
    lanes = msg.shape[2]
    hi = sq.astype(BF16).astype(F32)
    lo = sq - hi
    rows = [part[:, q * lanes : (q + 1) * lanes] for part in (hi, lo) for q in range(w // lanes)]
    if len(rows) < PAD:
        rows.append(jnp.zeros((PAD - len(rows), lanes), F32))
    msg[g, w : w + PAD, :] = jnp.concatenate(rows, axis=0).astype(BF16)


def get_squares(msg, g, w):
    tail = msg[g, w : w + PAD, :].astype(F32)
    count = w // msg.shape[2]
    rows = [tail[q : q + 1] + tail[count + q : count + q + 1] for q in range(count)]
    return jnp.concatenate(rows, axis=1)


def dipole_boundary_kernel(
    nblk, core, off, acc, x, intra, inter, t, d, sq, send, keep, total, *scratch
):
    groups, w, lanes = keep.shape
    bits = groups.bit_length() - 1
    total[...] = acc[...] + boundary_rows(
        nblk, core[0], off, x, intra, inter, t, d, *scratch
    )
    for g in range(groups):
        orders = [chip_order(bits, side) for side in (0, 1)]
        places = [
            sum(((g >> (bits - 1 - s)) & 1) << orders[side][s] for s in range(bits))
            for side in (0, 1)
        ]
        owned = [
            total[:, (2 * places[side] + side) * lanes : (2 * places[side] + side + 1) * lanes]
            for side in (0, 1)
        ]
        keep[g] = jnp.where(core[0] == 0, owned[0], owned[1])
        send[g, 0:w, :] = jnp.where(core[0] == 0, owned[1], owned[0]).astype(BF16)
        put_squares(send, g, sq[...], w)


def chip_order(bits, side):
    return [(s + side) % bits for s in range(bits)]


def dipole_boundary(core, off, acc, x, intra, inter, t, d, sq, groups):
    nblk, _, w = x.shape
    nt = t.shape[2]
    lanes = nt // (2 * groups)
    return pl.pallas_call(
        functools.partial(dipole_boundary_kernel, nblk),
        out_shape=(
            jax.ShapeDtypeStruct((groups, w + PAD, lanes), BF16),
            jax.ShapeDtypeStruct((groups, w, lanes), F32),
        ),
        in_specs=[SMEM, SMEM, VMEM, ANY, ANY, ANY, ANY, ANY, VMEM],
        out_specs=(VMEM, VMEM),
        scratch_shapes=[pltpu.VMEM((w, nt), F32)] + boundary_scratch(w, nt),
        compiler_params=params(),
        cost_estimate=cost(4 * BK * w * (KB * BK + nt), 8 * 2**20),
    )(core, off, acc, x, intra, inter, t, d, sq)


def halve_kernel(bit, keep, got, sq, send, kept, sq_out):
    half, w, _ = kept.shape
    total = sq[...] + get_squares(got, 0, w)
    sq_out[...] = total
    for g in range(half):
        here, there = bit[0] * half + g, (1 - bit[0]) * half + g
        kept[g] = keep[here] + got[here, 0:w, :].astype(F32)
        send[g, 0:w, :] = (keep[there] + got[there, 0:w, :].astype(F32)).astype(BF16)
        put_squares(send, g, total, w)


def halve(bit, keep, got, sq):
    groups, w, lanes = keep.shape
    half = groups // 2
    return pl.pallas_call(
        halve_kernel,
        out_shape=(
            jax.ShapeDtypeStruct((half, w + PAD, lanes), BF16),
            jax.ShapeDtypeStruct((half, w, lanes), F32),
            jax.ShapeDtypeStruct((1, w), F32),
        ),
        in_specs=[SMEM, VMEM, VMEM, VMEM],
        out_specs=(VMEM,) * 3,
        compiler_params=params(16),
    )(bit, keep, got, sq)


def finish_kernel(rows, keep, got, sq, out):
    w = keep.shape[1]
    total = sq[...] + get_squares(got, 0, w)
    norm = 1.0 / jnp.sqrt(total / rows + 1e-06)
    raw = keep[0] + got[0, 0:w, :].astype(F32)
    out[...] = (raw.T * norm).astype(BF16)


def finish(rows, keep, got, sq):
    _, w, lanes = keep.shape
    return pl.pallas_call(
        functools.partial(finish_kernel, rows),
        out_shape=jax.ShapeDtypeStruct((lanes, w), BF16),
        in_specs=[VMEM] * 3,
        out_specs=VMEM,
        compiler_params=params(16),
    )(keep, got, sq)


def swap(block, count, mask):
    return lax.ppermute(block, "basis", [(i, i ^ mask[i % 2]) for i in range(count)])


def meet(block, count):
    pairs = [(i, i + 1) for i in range(1, count - 1, 2)]
    return lax.ppermute(block, "basis", pairs + [(b, a) for a, b in pairs])


def on_device(cont_orbitals, target_orbitals, margin_blocks, dipole_blocks, band_offsets):
    count = lax.axis_size("basis")
    rows, w = cont_orbitals.shape
    nblk = rows // BK
    nt = target_orbitals.shape[1]
    chips = count // 2
    bits = chips.bit_length() - 1
    place = lax.axis_index("basis")
    core = lax.rem(place, 2)
    chip = lax.div(place, 2)
    core_s = core.astype(jnp.int32).reshape(1)
    off = band_offsets.astype(jnp.int32).T
    c = cont_orbitals.reshape(nblk, BK, w)
    t = target_orbitals.reshape(nblk, BK, nt)
    both = (1, 1)

    first, last = c[:2], c[nblk - 2 :]
    inter = meet(jnp.where(core == 0, first, last), count)
    intra = swap(jnp.where(core == 0, last, first), count, both)
    acc = project_interior(off, c, t, margin_blocks)
    send, keep = project_boundary(core_s, off, acc, c, intra, inter, t, margin_blocks)

    part = (keep + swap(send, count, both).astype(F32)).astype(BF16)
    orders = [chip_order(bits, side) for side in (0, 1)]
    for s in range(bits):
        got = swap(part, count, (2 << orders[0][s], 2 << orders[1][s]))
        part = (part.astype(F32) + got.astype(F32)).astype(BF16)
    other = swap(part, count, both)

    edge, intra_send, inter_send, sq = orth_edges(core_s, part, other, c, t)
    inter = meet(inter_send, count)
    intra = swap(intra_send, count, both)
    x, acc, sq = orth_dipole_interior(
        core_s, off, part, other, c, t, dipole_blocks, edge, sq
    )
    send, keep = dipole_boundary(
        core_s, off, acc, x, intra, inter, t, dipole_blocks, sq, chips
    )
    got = swap(send, count, both)
    for s in range(bits):
        which = jnp.where(core == 0, orders[0][s], orders[1][s])
        bit = jnp.bitwise_and(jnp.right_shift(chip, which), 1).astype(jnp.int32).reshape(1)
        send, keep, sq = halve(bit, keep, got, sq)
        got = swap(send, count, (2 << orders[0][s], 2 << orders[1][s]))
    dipole_mo = finish(rows * count, keep, got, sq)
    return (x.reshape(rows, w), dipole_mo)


def solution(mesh):
    return jax.shard_map(
        on_device,
        mesh=mesh,
        in_specs=(
            P("basis", "orb"),
            P("basis", None),
            P("basis", None, None, None),
            P("basis", None, None, None),
            P("basis", None),
        ),
        out_specs=(P("basis", "orb"), P("basis", "orb")),
        check_vma=False,
    )
```

```python
import functools

import jax
import jax.numpy as jnp
from jax import lax
from jax.experimental import pallas as pl
from jax.experimental.pallas import tpu as pltpu
from jax.sharding import PartitionSpec as P

BK = 256
KB = 4
F32 = jnp.float32
BF16 = jnp.bfloat16
ANY = pl.BlockSpec(memory_space=pl.ANY)
VMEM = pl.BlockSpec(memory_space=pltpu.VMEM)
SMEM = pl.BlockSpec(memory_space=pltpu.SMEM)


def core_of(place):
    return jnp.bitwise_and(place[0], 1)


def stay(x):
    return pltpu.with_memory_space_constraint(x, pltpu.HBM)


def params(mib=40):
    return pltpu.CompilerParams(vmem_limit_bytes=mib * 2**20)


def cost(macs, data):
    return pl.CostEstimate(flops=2 * macs, bytes_accessed=data, transcendentals=0)


def dot(a, b, dims=((1,), (0,))):
    return lax.dot_general(a, b, (dims, ((), ())), preferred_element_type=F32)


class Loads:
    def __init__(self, sems, ahead=64):
        self.sems, self.ahead = sems, ahead
        self.copies, self.started, self.done = [], 0, set()

    def start(self, src, dst):
        self.copies.append(pltpu.make_async_copy(src, dst, self.sems.at[len(self.copies)]))
        self.go()
        return len(self.copies) - 1

    def go(self):
        while self.started < min(len(self.copies), len(self.done) + self.ahead):
            self.copies[self.started].start()
            self.started += 1

    def wait(self, *which):
        for i in which:
            if i not in self.done:
                self.copies[i].wait()
                self.done.add(i)
                self.go()

    def wait_all(self):
        self.wait(*range(len(self.copies)))


def band_rows(rows, slots, off, field, cols, blocks, base, ys):
    for r, (b, slot) in enumerate(zip(rows, slots)):
        total = None
        for k in range(KB):
            term = dot(blocks[slot, k], field[b + off[k, b] + base, :, 0:cols])
            total = term if total is None else total + term
        ys[r * BK : (r + 1) * BK, :] = total.astype(BF16)


def groups_of(nblk):
    inner = list(range(2, nblk - 2))
    return [inner[i : i + 4] for i in range(0, len(inner), 4)]


def project(out, acc, ys, t_v, lo, count):
    size = count * BK
    t = t_v[lo : lo + count].reshape(size, -1)
    for at in range(0, out.shape[0], BK):
        here = slice(at, min(at + BK, out.shape[0]))
        piece = dot(ys[0:size, here], t, ((0,), (0,)))
        out[here, :] = piece if acc is None else acc[here, :] + piece


def columns(z, width):
    return pl.ds(pl.multiple_of(z * width, width), width)


def held(x):
    return pltpu.with_memory_space_constraint(x, pltpu.VMEM)


def edge_kernel(place, z, c, t, intra, inter, sems):
    last = c.shape[0] - 2
    w = c.shape[2]
    zc = intra.shape[2] - w
    loads = Loads(sems)
    for out, at in ((intra, (1 - core_of(place)) * last), (inter, core_of(place) * last)):
        loads.start(c.at[pl.ds(at, 2)], out.at[:, :, 0:w])
        loads.start(t.at[pl.ds(at, 2), :, columns(z[0], zc)], out.at[:, :, w : w + zc])
    loads.wait_all()


def edges(place, z, c, t, zc):
    _, _, w = c.shape
    pair = jax.ShapeDtypeStruct((2, BK, w + zc), BF16)
    return pl.pallas_call(
        edge_kernel,
        out_shape=(pair, pair),
        in_specs=[SMEM, SMEM, ANY, ANY],
        out_specs=(VMEM, VMEM),
        scratch_shapes=[pltpu.SemaphoreType.DMA((4,))],
        compiler_params=params(8),
    )(place, z, stay(c), stay(t))


def lead_of(nblk):
    groups = groups_of(nblk)
    cut = max(1, len(groups) - 1)
    return groups[:cut], groups[cut:]


def first_kernel(
    nblk, z, off, c, t, m, d, p_out, r_out, f, t_v, m_edge, m_v, d_v, ys, yd, sems
):
    w = c.shape[2]
    zc = f.shape[2] - w
    loads = Loads(sems, 8)
    groups = groups_of(nblk)
    lead, _ = lead_of(nblk)
    have, z_have, needs = 0, 0, []
    for g, rows in enumerate(groups):
        lo, hi = rows[0], rows[-1] + 1
        mid = min(lo + 2, hi)
        want = []
        for part in ((lo, mid), (mid, hi)):
            if part[0] == part[1]:
                continue
            upto = part[1] + 2
            ids = []
            if upto > have:
                ids.append(loads.start(c.at[have:upto], f.at[have:upto, :, 0:w]))
                have = upto
            ids.append(
                loads.start(m.at[part[0] : part[1]], m_v.at[part[0] - 2 : part[1] - 2])
            )
            want.append((list(range(*part)), ids))
        t_id = loads.start(t.at[lo:hi], t_v.at[lo:hi])
        d_ids = ()
        if g < len(lead):
            upto = hi + 2
            d_ids = (
                loads.start(d.at[lo:hi], d_v.at[lo - 2 : hi - 2]),
                loads.start(
                    t.at[z_have:upto, :, columns(z[0], zc)], f.at[z_have:upto, :, w : w + zc]
                ),
            )
            z_have = upto
        needs.append((rows, want, t_id, d_ids))
    if z_have < nblk:
        loads.start(t.at[z_have:nblk, :, columns(z[0], zc)], f.at[z_have:nblk, :, w : w + zc])
    for side, at in ((0, 0), (1, nblk - 2)):
        loads.start(t.at[at : at + 2], t_v.at[at : at + 2])
        loads.start(m.at[at : at + 2], m_edge.at[2 * side : 2 * side + 2])
    for g, (rows, want, t_id, d_ids) in enumerate(needs):
        at = 0
        for part, ids in want:
            loads.wait(*ids)
            band_rows(
                part, [b - 2 for b in part], off, f, w, m_v, 0,
                ys.at[at * BK : (at + len(part)) * BK],
            )
            at += len(part)
        loads.wait(t_id)
        project(p_out, None if g == 0 else p_out, ys, t_v, rows[0], len(rows))
        if d_ids:
            loads.wait(*d_ids)
            band_rows(rows, [b - 2 for b in rows], off, f, w + zc, d_v, 0, yd)
            project(r_out, None if g == 0 else r_out, yd, t_v, rows[0], len(rows))
    loads.ahead = 64
    loads.go()
    loads.wait_all()


def first(z, off, c, t, m, d, zc):
    nblk, _, w = c.shape
    nt = t.shape[2]
    inner = nblk - 4
    count = sum(map(len, lead_of(nblk)[0]))
    macs = inner * BK * w * (KB * BK + nt) + count * BK * (w + zc) * (KB * BK + nt)
    return pl.pallas_call(
        functools.partial(first_kernel, nblk),
        out_shape=(
            pltpu.VMEM((w, nt), F32),
            pltpu.VMEM((w + zc, nt), F32),
            pltpu.VMEM((nblk, BK, w + zc), BF16),
            pltpu.VMEM((nblk, BK, nt), BF16),
            pltpu.VMEM((4, KB, BK, BK), BF16),
        ),
        in_specs=[SMEM, SMEM, ANY, ANY, ANY, ANY],
        out_specs=(VMEM,) * 5,
        scratch_shapes=[
            pltpu.VMEM((inner, KB, BK, BK), BF16),
            pltpu.VMEM((count, KB, BK, BK), BF16),
            pltpu.VMEM((4 * BK, w), BF16),
            pltpu.VMEM((4 * BK, w + zc), BF16),
            pltpu.SemaphoreType.DMA((7 * len(groups_of(nblk)) + 5,)),
        ],
        compiler_params=params(17),
        cost_estimate=cost(macs, 30 * 2**20),
    )(z, off, stay(c), stay(t), stay(m), stay(d))


def boundary_start(nblk, core, f, intra, inter, f_v, sems):
    loads = Loads(sems)
    cols = f_v.shape[2]
    low = 10 * (1 - core)
    loads.start(intra.at[:, :, 0:cols], f_v.at[pl.ds(low, 2)])
    loads.start(inter.at[:, :, 0:cols], f_v.at[pl.ds(10 - low, 2)])
    loads.start(f.at[0:4, :, 0:cols], f_v.at[2:6])
    loads.start(f.at[nblk - 4 : nblk, :, 0:cols], f_v.at[6:10])
    return loads


def boundary_rows(nblk, loads, off, blocks, f_v, ys):
    cols = f_v.shape[2]
    loads.wait(0, 1, 2)
    band_rows([0, 1], [0, 1], off, f_v, cols, blocks, 2, ys.at[0 : 2 * BK])
    loads.wait(3)
    band_rows(
        [nblk - 2, nblk - 1], [2, 3], off, f_v, cols, blocks, 10 - nblk, ys.at[2 * BK : 4 * BK]
    )


def boundary_sum(acc, ys, t, here):
    nblk = t.shape[0]
    ends = ((0,), (0,))
    low = dot(ys[0 : 2 * BK, here], t[0:2].reshape(2 * BK, -1), ends)
    high = dot(ys[2 * BK : 4 * BK, here], t[nblk - 2 : nblk].reshape(2 * BK, -1), ends)
    return acc[here, :] + (low + high)


def boundary_scratch(cols):
    return [
        pltpu.VMEM((12, BK, cols), BF16),
        pltpu.VMEM((4 * BK, cols), BF16),
        pltpu.SemaphoreType.DMA((4,)),
    ]


def boundary_kernel(
    nblk, place, off, acc, f, intra, inter, t, m, d, send, keep, d_edge, d_rest, f_v, ys, sems, d_sems
):
    near = boundary_start(nblk, core_of(place), f, intra, inter, f_v, sems)
    loads = Loads(d_sems)
    _, rest = lead_of(nblk)
    if rest:
        loads.start(d.at[rest[0][0] : rest[-1][-1] + 1], d_rest)
    for side, at in ((0, 0), (1, nblk - 2)):
        loads.start(d.at[at : at + 2], d_edge.at[2 * side : 2 * side + 2])
    half = send.shape[0]
    boundary_rows(nblk, near, off, m, f_v, ys)
    here = pl.ds(pl.multiple_of(core_of(place) * half, half), half)
    there = pl.ds(pl.multiple_of((1 - core_of(place)) * half, half), half)
    send[...] = boundary_sum(acc, ys, t, there).astype(BF16)
    keep[...] = boundary_sum(acc, ys, t, here)
    loads.wait_all()


def project_boundary(place, off, acc, f, intra, inter, t, m, d):
    nblk, _, nt = t.shape
    w = acc.shape[0]
    others = sum(map(len, lead_of(nblk)[1]))
    return pl.pallas_call(
        functools.partial(boundary_kernel, nblk),
        out_shape=(
            jax.ShapeDtypeStruct((w // 2, nt), BF16),
            jax.ShapeDtypeStruct((w // 2, nt), F32),
            pltpu.VMEM((4, KB, BK, BK), BF16),
            pltpu.VMEM((max(others, 1), KB, BK, BK), BF16),
        ),
        in_specs=[SMEM, SMEM] + [VMEM] * 6 + [ANY],
        out_specs=(VMEM,) * 4,
        scratch_shapes=boundary_scratch(w) + [pltpu.SemaphoreType.DMA((3,))],
        compiler_params=params(10),
        cost_estimate=cost(4 * BK * w * (KB * BK + nt), 8 * 2**20),
    )(place, off, held(acc), held(f), intra, inter, held(t), held(m), stay(d))


def merge_kernel(passed, a, b, out, passed_on):
    out[...] = (a[...].astype(F32) + b[...].astype(F32)).astype(BF16)


def merge(passed, a, b):
    return pl.pallas_call(
        merge_kernel,
        out_shape=(
            jax.ShapeDtypeStruct(b.shape, BF16),
            jax.ShapeDtypeStruct(passed.shape, passed.dtype),
        ),
        in_specs=[ANY, VMEM, VMEM],
        out_specs=(VMEM, ANY),
        input_output_aliases={0: 1},
        compiler_params=params(8),
    )(passed, a, b)


def place_projection(core, mine, other, p):
    half = mine.shape[0]
    p[pl.ds(pl.multiple_of(core * half, half), half), :] = mine[...]
    p[pl.ds(pl.multiple_of((1 - core) * half, half), half), :] = other[...]


def square_sum(x):
    x = x.astype(F32)
    return jnp.sum(x * x, axis=0, keepdims=True)


def orth_rows(c, t, p):
    return (c.astype(F32) - dot(t, p, ((1,), (1,)))).astype(BF16)


def orth_kernel(part, place, mine, other, after, x_in, sq_in, f, t, x_out, sq, x_v, p, out_sems):
    nt = t.shape[2]
    w = sq.shape[1]
    stores = Loads(out_sems)
    lo, hi = part
    place_projection(core_of(place), mine, other, p)
    sq[...] = sq_in[...]
    for i, at in enumerate(range(lo, hi, 2)):
        block = f[at : at + 2, :, 0:w].reshape(2 * BK, w)
        x = orth_rows(block, t[at : at + 2].reshape(2 * BK, nt), p[...])
        x_v[2 * i : 2 * i + 2] = x.reshape(2, BK, w)
        sq[...] += square_sum(x)
        stores.start(x_v.at[2 * i : 2 * i + 2], x_out.at[at : at + 2])
    stores.wait_all()


def orthogonalize(part, place, mine, other, after, x, sq, f, t):
    nblk, _, nt = t.shape
    w = 2 * mine.shape[0]
    size = part[1] - part[0]
    return pl.pallas_call(
        functools.partial(orth_kernel, part),
        out_shape=(pltpu.HBM((nblk, BK, w), BF16), jax.ShapeDtypeStruct((1, w), F32)),
        in_specs=[SMEM, VMEM, VMEM, ANY, ANY, VMEM, VMEM, VMEM],
        out_specs=(ANY, VMEM),
        input_output_aliases={} if x is None else {4: 0},
        scratch_shapes=[
            pltpu.VMEM((size, BK, w), BF16),
            pltpu.VMEM((w, nt), BF16),
            pltpu.SemaphoreType.DMA((size // 2,)),
        ],
        compiler_params=params(7),
        cost_estimate=cost(size * BK * w * nt, 8 * 2**20),
    )(place, mine, other, after, after if x is None else x, sq, held(f), held(t))


def chip_order(bits, side):
    return [(s + side) % bits for s in range(bits)]


def dipole_rest_kernel(
    nblk, place, off, after, acc, f, intra, inter, t, d_edge, d_rest, send, keep, total, yd, f_v, ys, sems
):
    groups, cols, lanes = keep.shape
    bits = groups.bit_length() - 1
    near = boundary_start(nblk, core_of(place), f, intra, inter, f_v, sems)
    _, rest = lead_of(nblk)
    for g, rows in enumerate(rest):
        slot = rows[0] - rest[0][0]
        band_rows(rows, range(slot, slot + len(rows)), off, f, cols, d_rest, 0, yd)
        project(total, acc if g == 0 else total, yd, t, rows[0], len(rows))
    acc = total if rest else acc
    boundary_rows(nblk, near, off, d_edge, f_v, ys)
    orders = [chip_order(bits, side) for side in (0, 1)]
    for at in range(0, cols, BK):
        here = slice(at, min(at + BK, cols))
        whole = boundary_sum(acc, ys, t, here)
        for g in range(groups):
            owned = []
            for side in (0, 1):
                chip = sum(
                    ((g >> (bits - 1 - s)) & 1) << orders[side][s] for s in range(bits)
                )
                first_lane = (2 * chip + side) * lanes
                owned.append(whole[:, first_lane : first_lane + lanes])
            keep[g, here, :] = jnp.where(core_of(place) == 0, owned[0], owned[1])
            send[g, here, :] = jnp.where(core_of(place) == 0, owned[1], owned[0]).astype(BF16)


def dipole_rest(place, off, after, acc, f, intra, inter, t, d_edge, d_rest, groups):
    nblk, _, nt = t.shape
    cols = acc.shape[0]
    lanes = nt // (2 * groups)
    count = sum(map(len, lead_of(nblk)[1])) + 4
    return pl.pallas_call(
        functools.partial(dipole_rest_kernel, nblk),
        out_shape=(
            jax.ShapeDtypeStruct((groups, cols, lanes), BF16),
            jax.ShapeDtypeStruct((groups, cols, lanes), F32),
        ),
        in_specs=[SMEM, SMEM, ANY] + [VMEM] * 7,
        out_specs=(VMEM, VMEM),
        scratch_shapes=[pltpu.VMEM((cols, nt), F32), pltpu.VMEM((4 * BK, cols), BF16)]
        + boundary_scratch(cols),
        compiler_params=params(15),
        cost_estimate=cost(count * BK * cols * (KB * BK + nt), 8 * 2**20),
    )(place, off, after, held(acc), held(f), intra, inter, held(t), held(d_edge), held(d_rest))


def halve_kernel(step, place, after, keep, got, send, kept):
    half = kept.shape[0]
    orders = [chip_order(step[1], side)[step[0]] for side in (0, 1)]
    which = jnp.where(core_of(place) == 0, orders[0], orders[1])
    bit = jnp.bitwise_and(jnp.right_shift(place[0], which + 1), 1)
    for g in range(half):
        here, there = bit * half + g, (1 - bit) * half + g
        kept[g] = keep[here] + got[here].astype(F32)
        send[g] = (keep[there] + got[there].astype(F32)).astype(BF16)


def halve(step, place, after, keep, got):
    groups, cols, lanes = keep.shape
    half = groups // 2
    return pl.pallas_call(
        functools.partial(halve_kernel, step),
        out_shape=(
            jax.ShapeDtypeStruct((half, cols, lanes), BF16),
            jax.ShapeDtypeStruct((half, cols, lanes), F32),
        ),
        in_specs=[SMEM, ANY, VMEM, VMEM],
        out_specs=(VMEM,) * 2,
        compiler_params=params(8),
    )(place, after, keep, got)


def settle_kernel(w, after, keep, got, out):
    out[...] = (keep[0, w:, :] + got[0, w:, :].astype(F32)).astype(BF16)


def settle(w, after, keep, got):
    _, cols, lanes = keep.shape
    return pl.pallas_call(
        functools.partial(settle_kernel, w),
        out_shape=jax.ShapeDtypeStruct((cols - w, lanes), BF16),
        in_specs=[ANY, VMEM, VMEM],
        out_specs=VMEM,
        compiler_params=params(8),
    )(after, keep, got)


def stack_kernel(after, *refs):
    out, at = refs[-1], 0
    for piece in refs[:-1]:
        out[at : at + piece.shape[0], :] = piece[...]
        at += piece.shape[0]


def stack(after, pieces):
    rows = sum(piece.shape[0] for piece in pieces)
    return pl.pallas_call(
        stack_kernel,
        out_shape=jax.ShapeDtypeStruct((rows, pieces[0].shape[1]), BF16),
        in_specs=[ANY] + [VMEM] * len(pieces),
        out_specs=VMEM,
        compiler_params=params(8),
    )(after, *pieces)


def finish_kernel(rows, place, z, keep, got, mine, other, sq, *refs):
    pieces, (out, g_v) = refs[:-2], refs[-2:]
    half, w = mine.shape[0], sq.shape[1]
    zc = keep.shape[1] - w
    at = 0
    for piece in pieces:
        for q in range(piece.shape[0] // zc):
            where = pl.multiple_of(jnp.bitwise_xor(z[0], at) * zc, zc)
            g_v[pl.ds(where, zc), :] = piece[q * zc : (q + 1) * zc, :]
            at += 1
    norm = 1.0 / jnp.sqrt(sq[...] / rows + 1e-06)
    for side in (0, 1):
        here = slice(side * half, (side + 1) * half)
        p = jnp.where(core_of(place) == side, mine[...], other[...])
        raw = keep[0, here, :] + got[0, here, :].astype(F32) - dot(p, g_v[...])
        out[:, here] = (raw.T * norm[:, here]).astype(BF16)


def finish(rows, place, z, keep, got, mine, other, sq, pieces):
    _, cols, lanes = keep.shape
    nt = mine.shape[1]
    w = sq.shape[1]
    return pl.pallas_call(
        functools.partial(finish_kernel, rows),
        out_shape=jax.ShapeDtypeStruct((lanes, w), BF16),
        in_specs=[SMEM, SMEM] + [VMEM] * (5 + len(pieces)),
        out_specs=VMEM,
        scratch_shapes=[pltpu.VMEM((nt, lanes), BF16)],
        compiler_params=params(8),
    )(place, z, keep, got, mine, other, sq, *pieces)


def swap(block, count, mask):
    return lax.ppermute(block, "basis", [(i, i ^ mask[i % 2]) for i in range(count)])


def meet(block, count):
    pairs = [(i, i + 1) for i in range(1, count - 1, 2)]
    return lax.ppermute(block, "basis", pairs + [(b, a) for a, b in pairs])


def exchange(intra, inter, count):
    inter = meet(inter, count)
    return swap(intra, count, (1, 1)), inter


def scalar(x):
    return x.astype(jnp.int32).reshape(1)


def on_device(cont_orbitals, target_orbitals, margin_blocks, dipole_blocks, band_offsets):
    count = lax.axis_size("basis")
    planes = lax.axis_size("orb")
    rows, w = cont_orbitals.shape
    nblk = rows // BK
    nt = target_orbitals.shape[1]
    zc = nt // planes
    chips = count // 2
    bits = chips.bit_length() - 1
    place_s = scalar(lax.axis_index("basis"))
    z = lax.axis_index("orb")
    z_s = scalar(z)
    off = band_offsets.astype(jnp.int32).T
    c = cont_orbitals.reshape(nblk, BK, w)
    t = target_orbitals.reshape(nblk, BK, nt)
    zero = jnp.zeros((1, w), F32)
    both = (1, 1)
    orders = [chip_order(bits, side) for side in (0, 1)]
    masks = [(2 << orders[0][s], 2 << orders[1][s]) for s in range(bits)]

    intra, inter = exchange(*edges(place_s, z_s, c, t, zc), count)
    p_acc, r_acc, f, t_v, m_edge = first(z_s, off, c, t, margin_blocks, dipole_blocks, zc)
    send, keep, d_edge, d_rest = project_boundary(
        place_s, off, p_acc, f, intra, inter, t_v, m_edge, dipole_blocks
    )
    part, r_acc = merge(r_acc, keep, swap(send, count, both))

    got = swap(part, count, masks[0])
    send, keep = dipole_rest(
        place_s, off, part, r_acc, f, intra, inter, t_v, d_edge, d_rest, chips
    )
    part, send = merge(send, part, got)
    for s in range(1, bits):
        got = swap(part, count, masks[s])
        got_r = swap(send, count, both if s == 1 else masks[s - 2])
        send, keep = halve((s - 1, bits), place_s, part, keep, got_r)
        part, send = merge(send, part, got)
    other = swap(part, count, both)
    got_r = swap(send, count, masks[bits - 2])

    half = nblk // 4 * 2
    x, sq = orthogonalize((0, half), place_s, part, other, part, None, zero, f, t_v)
    send, keep = halve((bits - 1, bits), place_s, sq, keep, got_r)
    got_r = swap(send, count, masks[bits - 1])
    x, sq = orthogonalize((half, nblk), place_s, part, other, send, x, sq, f, t_v)
    pieces = [settle(w, sq, keep, got_r)]
    tail = [both] + masks
    step = 1
    while step < planes or tail:
        if tail:
            sq = sq + swap(sq, count, tail.pop(0))
        if step < planes:
            whole = pieces[0] if step == 1 else stack(sq, pieces)
            pieces.append(lax.ppermute(whole, "orb", [(i, i ^ step) for i in range(planes)]))
            step *= 2
    dipole_mo = finish(rows * count, place_s, z_s, keep, got_r, part, other, sq, pieces)
    return (x.reshape(rows, w), dipole_mo)


def solution(mesh):
    return jax.shard_map(
        on_device,
        mesh=mesh,
        in_specs=(
            P("basis", "orb"),
            P("basis", None),
            P("basis", None, None, None),
            P("basis", None, None, None),
            P("basis", None),
        ),
        out_specs=(P("basis", "orb"), P("basis", "orb")),
        check_vma=False,
    )
```

```python
import functools

import jax
import jax.numpy as jnp
from jax import lax
from jax.experimental import pallas as pl
from jax.experimental.pallas import tpu as pltpu
from jax.sharding import PartitionSpec as P

BK = 256
KB = 4
LEAD = 2
F32 = jnp.float32
BF16 = jnp.bfloat16
ANY = pl.BlockSpec(memory_space=pl.ANY)
VMEM = pl.BlockSpec(memory_space=pltpu.VMEM)
SMEM = pl.BlockSpec(memory_space=pltpu.SMEM)


def core_of(place):
    return jnp.bitwise_and(place[0], 1)


def stay(x):
    return pltpu.with_memory_space_constraint(x, pltpu.HBM)


def params(mib=40):
    return pltpu.CompilerParams(vmem_limit_bytes=mib * 2**20)


def cost(macs, data):
    return pl.CostEstimate(flops=2 * macs, bytes_accessed=data, transcendentals=0)


def dot(a, b, dims=((1,), (0,))):
    return lax.dot_general(a, b, (dims, ((), ())), preferred_element_type=F32)


class Loads:
    def __init__(self, sems, ahead=64):
        self.sems, self.ahead = sems, ahead
        self.copies, self.started, self.done = [], 0, set()

    def start(self, src, dst):
        self.copies.append(pltpu.make_async_copy(src, dst, self.sems.at[len(self.copies)]))
        self.go()
        return len(self.copies) - 1

    def go(self):
        while self.started < min(len(self.copies), len(self.done) + self.ahead):
            self.copies[self.started].start()
            self.started += 1

    def wait(self, *which):
        for i in which:
            if i not in self.done:
                self.copies[i].wait()
                self.done.add(i)
                self.go()

    def wait_all(self):
        self.wait(*range(len(self.copies)))


def band_rows(rows, slots, off, field, cols, blocks, base, ys, at=0):
    for r, (b, slot) in enumerate(zip(rows, slots)):
        total = None
        for k in range(KB):
            term = dot(blocks[slot, k], field[b + off[k, b] + base, :, 0:cols])
            total = term if total is None else total + term
        ys[r * BK : (r + 1) * BK, at : at + cols] = total.astype(BF16)


def groups_of(nblk):
    inner = list(range(2, nblk - 2))
    return [inner[i : i + 4] for i in range(0, len(inner), 4)]


def project(out, acc, ys, t_v, lo, count):
    size = count * BK
    t = t_v[lo : lo + count].reshape(size, -1)
    for at in range(0, out.shape[0], BK):
        here = slice(at, min(at + BK, out.shape[0]))
        piece = dot(ys[0:size, here], t, ((0,), (0,)))
        out[here, :] = piece if acc is None else acc[here, :] + piece


def columns(z, width):
    return pl.ds(pl.multiple_of(z * width, width), width)


def held(x):
    return pltpu.with_memory_space_constraint(x, pltpu.VMEM)


def edge_kernel(place, c, intra, inter, sems):
    last = c.shape[0] - 2
    loads = Loads(sems)
    loads.start(c.at[pl.ds(core_of(place) * last, 2)], inter)
    loads.start(c.at[pl.ds((1 - core_of(place)) * last, 2)], intra)
    loads.wait_all()


def edges(place, c):
    pair = jax.ShapeDtypeStruct((2,) + c.shape[1:], BF16)
    return pl.pallas_call(
        edge_kernel,
        out_shape=(pair, pair),
        in_specs=[SMEM, ANY],
        out_specs=(VMEM, VMEM),
        scratch_shapes=[pltpu.SemaphoreType.DMA((2,))],
        compiler_params=params(8),
    )(place, stay(c))


def lead_of(nblk):
    inner = list(range(2, nblk - 2))
    rest = inner[LEAD:]
    return inner[:LEAD], [rest[i : i + 4] for i in range(0, len(rest), 4)]


def first_kernel(
    nblk, z, off, c, t, m, d, p_out, r_out, f, t_v, m_edge, m_v, d_v, ys, yd, sems
):
    w = c.shape[2]
    zc = f.shape[2] - w
    loads = Loads(sems, 8)
    lead, _ = lead_of(nblk)
    have, needs = 0, []
    for g, rows in enumerate(groups_of(nblk)):
        lo, hi = rows[0], rows[-1] + 1
        mid = min(lo + 2, hi)
        want = []
        for part in ((lo, mid), (mid, hi)):
            if part[0] == part[1]:
                continue
            upto = part[1] + 2
            ids = []
            if upto > have:
                ids.append(loads.start(c.at[have:upto], f.at[have:upto, :, 0:w]))
                have = upto
            ids.append(
                loads.start(m.at[part[0] : part[1]], m_v.at[part[0] - 2 : part[1] - 2])
            )
            want.append((list(range(*part)), ids))
        t_id = loads.start(t.at[lo:hi], t_v.at[lo:hi])
        d_ids = ()
        if g == 0:
            near = lead[-1] + 3
            d_ids = (
                loads.start(d.at[lead[0] : lead[-1] + 1], d_v),
                loads.start(t.at[0:near, :, columns(z[0], zc)], f.at[0:near, :, w : w + zc]),
            )
        needs.append((rows, want, t_id, d_ids))
    for side, at in ((0, 0), (1, nblk - 2)):
        loads.start(m.at[at : at + 2], m_edge.at[2 * side : 2 * side + 2])
        loads.start(t.at[at : at + 2], t_v.at[at : at + 2])
    loads.start(t.at[near:nblk, :, columns(z[0], zc)], f.at[near:nblk, :, w : w + zc])
    for g, (rows, want, t_id, d_ids) in enumerate(needs):
        at = 0
        for part, ids in want:
            loads.wait(*ids)
            band_rows(
                part, [b - 2 for b in part], off, f, w, m_v, 0,
                ys.at[at * BK : (at + len(part)) * BK],
            )
            at += len(part)
        loads.wait(t_id)
        project(p_out, None if g == 0 else p_out, ys, t_v, rows[0], len(rows))
        if d_ids:
            loads.wait(*d_ids)
            band_rows(lead, range(len(lead)), off, f, w + zc, d_v, 0, yd)
            project(r_out, None, yd, t_v, lead[0], len(lead))
        if g == 1:
            loads.ahead = 64
            loads.go()
    loads.wait_all()


def first(z, off, c, t, m, d, zc):
    nblk, _, w = c.shape
    nt = t.shape[2]
    inner = nblk - 4
    count = len(lead_of(nblk)[0])
    macs = inner * BK * w * (KB * BK + nt) + count * BK * (w + zc) * (KB * BK + nt)
    return pl.pallas_call(
        functools.partial(first_kernel, nblk),
        out_shape=(
            pltpu.VMEM((w, nt), F32),
            pltpu.VMEM((w + zc, nt), F32),
            pltpu.VMEM((nblk, BK, w + zc), BF16),
            pltpu.VMEM((nblk, BK, nt), BF16),
            pltpu.VMEM((4, KB, BK, BK), BF16),
        ),
        in_specs=[SMEM, SMEM, ANY, ANY, ANY, ANY],
        out_specs=(VMEM,) * 5,
        scratch_shapes=[
            pltpu.VMEM((inner, KB, BK, BK), BF16),
            pltpu.VMEM((count, KB, BK, BK), BF16),
            pltpu.VMEM((4 * BK, w), BF16),
            pltpu.VMEM((count * BK, w + zc), BF16),
            pltpu.SemaphoreType.DMA((5 * len(groups_of(nblk)) + 7,)),
        ],
        compiler_params=params(15),
        cost_estimate=cost(macs, 30 * 2**20),
    )(z, off, stay(c), stay(t), stay(m), stay(d))


def middle_kernel(groups, off, after, acc, f, t, d, d_rest, out, d_edge, yd, sems):
    nblk = f.shape[0]
    loads = Loads(sems)
    for side, at in ((0, 0), (1, nblk - 2)):
        loads.start(d.at[at : at + 2], d_edge.at[2 * side : 2 * side + 2])
    for g, rows in enumerate(groups):
        slot = rows[0] - groups[0][0]
        band_rows(rows, range(slot, slot + len(rows)), off, f, f.shape[2], d_rest, 0, yd)
        project(out, acc if g == 0 else out, yd, t, rows[0], len(rows))
    loads.wait_all()


def middle(off, after, acc, f, t, d, d_rest):
    nblk, _, cols = f.shape
    nt = t.shape[2]
    groups = lead_of(nblk)[1]
    count = sum(map(len, groups))
    return pl.pallas_call(
        functools.partial(middle_kernel, groups),
        out_shape=(pltpu.VMEM((cols, nt), F32), pltpu.VMEM((4, KB, BK, BK), BF16)),
        in_specs=[SMEM, ANY, VMEM, VMEM, VMEM, ANY, VMEM],
        out_specs=(VMEM, VMEM),
        scratch_shapes=[
            pltpu.VMEM((4 * BK, cols), BF16),
            pltpu.SemaphoreType.DMA((2,)),
        ],
        compiler_params=params(6),
        cost_estimate=cost(count * BK * cols * (KB * BK + nt), 14 * 2**20),
    )(off, after, held(acc), held(f), held(t), stay(d), held(d_rest))


def boundary_start(nblk, core, f, cols, intra, inter, f_v, sems):
    loads = Loads(sems)
    low = 10 * (1 - core)
    loads.start(f.at[0:4, :, cols], f_v.at[2:6])
    loads.start(intra, f_v.at[pl.ds(low, 2)])
    loads.start(inter, f_v.at[pl.ds(10 - low, 2)])
    loads.start(f.at[nblk - 4 : nblk, :, cols], f_v.at[6:10])
    return loads


def boundary_rows(nblk, loads, off, blocks, f_v, ys, at=0):
    cols = f_v.shape[2]
    if loads:
        loads.wait(0, 1, 2)
    band_rows([0, 1], [0, 1], off, f_v, cols, blocks, 2, ys.at[0 : 2 * BK], at)
    if loads:
        loads.wait(3)
    band_rows(
        [nblk - 2, nblk - 1], [2, 3], off, f_v, cols, blocks, 10 - nblk, ys.at[2 * BK : 4 * BK], at
    )


def boundary_sum(acc, ys, t, here):
    nblk = t.shape[0]
    ends = ((0,), (0,))
    low = dot(ys[0 : 2 * BK, here], t[0:2].reshape(2 * BK, -1), ends)
    high = dot(ys[2 * BK : 4 * BK, here], t[nblk - 2 : nblk].reshape(2 * BK, -1), ends)
    return acc[here, :] + (low + high)


def boundary_kernel(
    nblk, place, off, acc, f, intra, inter, t, m, d,
    send, keep, tz_intra, tz_inter, d_rest, f_v, ys, sems, d_sems,
):
    core = core_of(place)
    w = intra.shape[2]
    near = boundary_start(nblk, core, f, slice(0, w), intra, inter, f_v, sems)
    loads = Loads(d_sems)
    _, rest = lead_of(nblk)
    last = nblk - 2
    loads.start(f.at[pl.ds(core * last, 2), :, w:], tz_inter)
    loads.start(f.at[pl.ds((1 - core) * last, 2), :, w:], tz_intra)
    loads.start(d.at[rest[0][0] : rest[-1][-1] + 1], d_rest)
    half = send.shape[0]
    boundary_rows(nblk, near, off, m, f_v, ys)
    here = pl.ds(pl.multiple_of(core * half, half), half)
    there = pl.ds(pl.multiple_of((1 - core) * half, half), half)
    send[...] = boundary_sum(acc, ys, t, there).astype(BF16)
    keep[...] = boundary_sum(acc, ys, t, here)
    loads.wait_all()


def project_boundary(place, off, acc, f, intra, inter, t, m, d):
    nblk, _, nt = t.shape
    w = acc.shape[0]
    zc = f.shape[2] - w
    others = sum(map(len, lead_of(nblk)[1]))
    return pl.pallas_call(
        functools.partial(boundary_kernel, nblk),
        out_shape=(
            jax.ShapeDtypeStruct((w // 2, nt), BF16),
            jax.ShapeDtypeStruct((w // 2, nt), F32),
            jax.ShapeDtypeStruct((2, BK, zc), BF16),
            jax.ShapeDtypeStruct((2, BK, zc), BF16),
            pltpu.VMEM((others, KB, BK, BK), BF16),
            pltpu.VMEM((12, BK, w), BF16),
        ),
        in_specs=[SMEM, SMEM] + [VMEM] * 6 + [ANY],
        out_specs=(VMEM,) * 6,
        scratch_shapes=[
            pltpu.VMEM((4 * BK, w), BF16),
            pltpu.SemaphoreType.DMA((4,)),
            pltpu.SemaphoreType.DMA((3,)),
        ],
        compiler_params=params(10),
        cost_estimate=cost(4 * BK * w * (KB * BK + nt), 8 * 2**20),
    )(place, off, held(acc), held(f), intra, inter, held(t), held(m), stay(d))


def merge_kernel(after, a, b, out, *_):
    out[...] = (a[...].astype(F32) + b[...].astype(F32)).astype(BF16)


def merge(after, a, b, hold=False):
    shapes = [jax.ShapeDtypeStruct(b.shape, BF16)]
    if hold:
        shapes.append(jax.ShapeDtypeStruct(after.shape, after.dtype))
    out = pl.pallas_call(
        merge_kernel,
        out_shape=shapes,
        in_specs=[ANY, VMEM, VMEM],
        out_specs=[VMEM, ANY][: len(shapes)],
        input_output_aliases={0: 1} if hold else {},
        compiler_params=params(8),
    )(after, a, b)
    return out if hold else out[0]


def square_sum(x):
    x = x.astype(F32)
    return jnp.sum(x * x, axis=0, keepdims=True)


def orth_rows(c, t, p):
    return (c.astype(F32) - dot(t, p, ((1,), (1,)))).astype(BF16)


def orth_kernel(own, part, place, p, after, x_in, sq_in, f, t, x_out, sq, x_v, out_sems):
    nblk, _, nt = t.shape
    half = p.shape[0]
    core = core_of(place)
    side = core if own else 1 - core
    here = pl.ds(pl.multiple_of(side * half, half), half)
    stores = Loads(out_sems)
    total = None
    for at in range(part[0], part[1], 2):
        block = f[at : at + 2, :, here].reshape(2 * BK, half)
        x = orth_rows(block, t[at : at + 2].reshape(2 * BK, nt), p[...])
        x_v[at : at + 2] = x.reshape(2, BK, half)
        squares = square_sum(x)
        total = squares if total is None else total + squares
        stores.start(x_v.at[at : at + 2], x_out.at[at : at + 2, :, here])
    sq[...] = sq_in[...]
    sq[:, here] += total
    stores.wait_all()


def orthogonalize(own, part, place, p, after, x, sq, f, t):
    nblk, _, nt = t.shape
    half = p.shape[0]
    w = 2 * half
    return pl.pallas_call(
        functools.partial(orth_kernel, own, part),
        out_shape=(pltpu.HBM((nblk, BK, w), BF16), jax.ShapeDtypeStruct((1, w), F32)),
        in_specs=[SMEM, VMEM, ANY, ANY, VMEM, VMEM, VMEM],
        out_specs=(ANY, VMEM),
        input_output_aliases={} if x is None else {3: 0},
        scratch_shapes=[
            pltpu.VMEM((nblk, BK, half), BF16),
            pltpu.SemaphoreType.DMA((nblk // 2,)),
        ],
        compiler_params=params(7),
        cost_estimate=cost(nblk * BK * half * nt, 8 * 2**20),
    )(place, p, after, after if x is None else x, sq, held(f), held(t))


def chip_order(bits, side):
    return [(s + side) % bits for s in range(bits)]


def dipole_boundary_kernel(
    nblk, place, off, after, acc, f, near, tz_intra, tz_inter, t, d, send_0, send_1, keep, f_v, ys, sems
):
    groups, cols, lanes = keep.shape
    w = near.shape[2]
    bits = groups.bit_length() - 1
    loads = boundary_start(
        nblk, core_of(place), f, slice(w, cols), tz_intra, tz_inter, f_v, sems
    )
    boundary_rows(nblk, None, off, d, near, ys)
    boundary_rows(nblk, loads, off, d, f_v, ys, w)
    orders = [chip_order(bits, side) for side in (0, 1)]
    for at in range(0, cols, BK):
        here = slice(at, min(at + BK, cols))
        whole = boundary_sum(acc, ys, t, here)
        for g in range(groups):
            owned = []
            for side in (0, 1):
                chip = sum(
                    ((g >> (bits - 1 - s)) & 1) << orders[side][s] for s in range(bits)
                )
                first_lane = (2 * chip + side) * lanes
                owned.append(whole[:, first_lane : first_lane + lanes])
            keep[g, here, :] = jnp.where(core_of(place) == 0, owned[0], owned[1])
            send = (send_0, send_1)[2 * g // groups]
            away = jnp.where(core_of(place) == 0, owned[1], owned[0])
            send[g % (groups // 2), here, :] = away.astype(BF16)


def dipole_boundary(place, off, after, acc, f, near, tz, t, d, groups):
    nblk, _, nt = t.shape
    cols = acc.shape[0]
    lanes = nt // (2 * groups)
    return pl.pallas_call(
        functools.partial(dipole_boundary_kernel, nblk),
        out_shape=(
            jax.ShapeDtypeStruct((groups // 2, cols, lanes), BF16),
            jax.ShapeDtypeStruct((groups // 2, cols, lanes), BF16),
            jax.ShapeDtypeStruct((groups, cols, lanes), F32),
        ),
        in_specs=[SMEM, SMEM, ANY] + [VMEM] * 7,
        out_specs=(VMEM,) * 3,
        scratch_shapes=[
            pltpu.VMEM((12, BK, tz[0].shape[2]), BF16),
            pltpu.VMEM((4 * BK, cols), BF16),
            pltpu.SemaphoreType.DMA((4,)),
        ],
        compiler_params=params(9),
        cost_estimate=cost(4 * BK * cols * (KB * BK + nt), 8 * 2**20),
    )(place, off, after, held(acc), held(f), held(near), *tz, held(t), held(d))


def halve_kernel(step, place, after, keep, *refs):
    got, (send, kept) = refs[:-2], refs[-2:]
    half = kept.shape[0]
    orders = [chip_order(step[1], side)[step[0]] for side in (0, 1)]
    which = jnp.where(core_of(place) == 0, orders[0], orders[1])
    bit = jnp.bitwise_and(jnp.right_shift(place[0], which + 1), 1)

    def come(of, g):
        if len(got) == 1:
            return got[0][of * half + g].astype(F32)
        return jnp.where(of == 0, got[0][g], got[1][g]).astype(F32)

    for g in range(half):
        kept[g] = keep[bit * half + g] + come(bit, g)
        send[g] = (keep[(1 - bit) * half + g] + come(1 - bit, g)).astype(BF16)


def halve(step, place, after, keep, got):
    groups, cols, lanes = keep.shape
    half = groups // 2
    return pl.pallas_call(
        functools.partial(halve_kernel, step),
        out_shape=(
            jax.ShapeDtypeStruct((half, cols, lanes), BF16),
            jax.ShapeDtypeStruct((half, cols, lanes), F32),
        ),
        in_specs=[SMEM, ANY, VMEM] + [VMEM] * len(got),
        out_specs=(VMEM,) * 2,
        compiler_params=params(8),
    )(place, after, keep, *got)


def settle_kernel(w, after, keep, got, out):
    out[...] = (keep[0, w:, :] + got[0, w:, :].astype(F32)).astype(BF16)


def settle(w, after, keep, got):
    _, cols, lanes = keep.shape
    return pl.pallas_call(
        functools.partial(settle_kernel, w),
        out_shape=jax.ShapeDtypeStruct((cols - w, lanes), BF16),
        in_specs=[ANY, VMEM, VMEM],
        out_specs=VMEM,
        compiler_params=params(8),
    )(after, keep, got)


def stack_kernel(after, *refs):
    out, at = refs[-1], 0
    for piece in refs[:-1]:
        out[at : at + piece.shape[0], :] = piece[...]
        at += piece.shape[0]


def stack(after, pieces):
    rows = sum(piece.shape[0] for piece in pieces)
    return pl.pallas_call(
        stack_kernel,
        out_shape=jax.ShapeDtypeStruct((rows, pieces[0].shape[1]), BF16),
        in_specs=[ANY] + [VMEM] * len(pieces),
        out_specs=VMEM,
        compiler_params=params(8),
    )(after, *pieces)


def finish_kernel(rows, spots, place, z, keep, got, mine, other, sq, *refs):
    pieces, (out, g_v) = refs[:-2], refs[-2:]
    half, w = mine.shape[0], sq.shape[1]
    zc = keep.shape[1] - w
    at = 0
    for piece in pieces:
        for q in range(piece.shape[0] // zc):
            where = pl.multiple_of(jnp.bitwise_xor(z[0], spots[at]) * zc, zc)
            g_v[pl.ds(where, zc), :] = piece[q * zc : (q + 1) * zc, :]
            at += 1
    norm = 1.0 / jnp.sqrt(sq[...] / rows + 1e-06)
    for side in (0, 1):
        here = slice(side * half, (side + 1) * half)
        p = jnp.where(core_of(place) == side, mine[...], other[...])
        raw = keep[0, here, :] + got[0, here, :].astype(F32) - dot(p, g_v[...])
        out[:, here] = (raw.T * norm[:, here]).astype(BF16)


def finish(rows, spots, place, z, keep, got, mine, other, sq, pieces):
    _, cols, lanes = keep.shape
    nt = mine.shape[1]
    w = sq.shape[1]
    return pl.pallas_call(
        functools.partial(finish_kernel, rows, spots),
        out_shape=jax.ShapeDtypeStruct((lanes, w), BF16),
        in_specs=[SMEM, SMEM] + [VMEM] * (5 + len(pieces)),
        out_specs=VMEM,
        scratch_shapes=[pltpu.VMEM((nt, lanes), BF16)],
        compiler_params=params(8),
    )(place, z, keep, got, mine, other, sq, *pieces)


def swap(block, count, mask):
    return lax.ppermute(block, "basis", [(i, i ^ mask[i % 2]) for i in range(count)])


def meet(block, count):
    pairs = [(i, i + 1) for i in range(1, count - 1, 2)]
    return lax.ppermute(block, "basis", pairs + [(b, a) for a, b in pairs])


def exchange(intra, inter, count):
    inter = meet(inter, count)
    return swap(intra, count, (1, 1)), inter


def scalar(x):
    return x.astype(jnp.int32).reshape(1)


def on_device(cont_orbitals, target_orbitals, margin_blocks, dipole_blocks, band_offsets):
    count = lax.axis_size("basis")
    planes = lax.axis_size("orb")
    rows, w = cont_orbitals.shape
    nblk = rows // BK
    nt = target_orbitals.shape[1]
    zc = nt // planes
    chips = count // 2
    bits = chips.bit_length() - 1
    place_s = scalar(lax.axis_index("basis"))
    z = lax.axis_index("orb")
    z_s = scalar(z)
    off = band_offsets.astype(jnp.int32).T
    c = cont_orbitals.reshape(nblk, BK, w)
    t = target_orbitals.reshape(nblk, BK, nt)
    zero = jnp.zeros((1, w), F32)
    both = (1, 1)
    orders = [chip_order(bits, side) for side in (0, 1)]
    masks = [(2 << orders[0][s], 2 << orders[1][s]) for s in range(bits)]

    halos = exchange(*edges(place_s, c), count)
    p_acc, r_acc, f, t_v, m_edge = first(z_s, off, c, t, margin_blocks, dipole_blocks, zc)
    send, keep, *tz, d_rest, near = project_boundary(
        place_s, off, p_acc, f, *halos, t_v, m_edge, dipole_blocks
    )
    tz = exchange(*tz, count)
    part, r_acc = merge(r_acc, keep, swap(send, count, both), hold=True)

    for s in range(bits):
        got = swap(part, count, masks[s])
        if s == 0:
            r_acc, d_edge = middle(off, part, r_acc, f, t_v, dipole_blocks, d_rest)
            part, r_acc = merge(r_acc, part, got, hold=True)
            continue
        if s == 1:
            *sends, keep = dipole_boundary(
                place_s, off, part, r_acc, f, near, tz, t_v, d_edge, chips
            )
            got_r = [swap(send, count, both) for send in sends]
            send = sends[0]
        else:
            send, keep = halve((s - 2, bits), place_s, part, keep, got_r)
            got_r = [swap(send, count, masks[s - 2])]
        part = merge(send, part, got)
    other = swap(part, count, both)
    send, keep = halve((bits - 2, bits), place_s, part, keep, got_r)
    got_r = [swap(send, count, masks[bits - 2])]

    half = nblk // 4 * 2
    x, sq = orthogonalize(True, (0, nblk), place_s, part, part, None, zero, f, t_v)
    x, sq = orthogonalize(False, (0, half), place_s, other, part, x, sq, f, t_v)
    send, keep = halve((bits - 1, bits), place_s, sq, keep, got_r)
    got_r = [swap(send, count, masks[bits - 1])]
    x, sq = orthogonalize(False, (half, nblk), place_s, other, send, x, sq, f, t_v)
    tail = [both] + masks
    sq = sq + swap(sq, count, tail.pop(0))
    pieces = [settle(w, sq, keep, got_r[0])]
    spots, step = [0], planes // 2
    while step:
        whole = pieces[0]
        if len(pieces) > 1:
            if tail:
                sq = sq + swap(sq, count, tail.pop(0))
            whole = stack(sq, pieces)
        pieces.append(lax.ppermute(whole, "orb", [(i, i ^ step) for i in range(planes)]))
        spots += [spot ^ step for spot in spots]
        step //= 2
    for mask in tail:
        sq = sq + swap(sq, count, mask)
    dipole_mo = finish(rows * count, spots, place_s, z_s, keep, got_r[0], part, other, sq, pieces)
    return (x.reshape(rows, w), dipole_mo)


def solution(mesh):
    return jax.shard_map(
        on_device,
        mesh=mesh,
        in_specs=(
            P("basis", "orb"),
            P("basis", None),
            P("basis", None, None, None),
            P("basis", None, None, None),
            P("basis", None),
        ),
        out_specs=(P("basis", "orb"), P("basis", "orb")),
        check_vma=False,
    )
```

```python
import functools

import jax
import jax.numpy as jnp
from jax import lax
from jax.experimental import pallas as pl
from jax.experimental.pallas import tpu as pltpu
from jax.sharding import PartitionSpec as P

BK = 256
KB = 4
LEAD = 1
LAST = 2
MOST = 5
F32 = jnp.float32
BF16 = jnp.bfloat16
ANY = pl.BlockSpec(memory_space=pl.ANY)
VMEM = pl.BlockSpec(memory_space=pltpu.VMEM)
SMEM = pl.BlockSpec(memory_space=pltpu.SMEM)


def core_of(place):
    return jnp.bitwise_and(place[0], 1)


def stay(x):
    return pltpu.with_memory_space_constraint(x, pltpu.HBM)


def params(mib=40):
    return pltpu.CompilerParams(vmem_limit_bytes=mib * 2**20)


def cost(macs, data):
    return pl.CostEstimate(flops=2 * macs, bytes_accessed=data, transcendentals=0)


def dot(a, b, dims=((1,), (0,))):
    return lax.dot_general(a, b, (dims, ((), ())), preferred_element_type=F32)


class Loads:
    def __init__(self, sems, ahead=64):
        self.sems, self.ahead = sems, ahead
        self.copies, self.started, self.done = [], 0, set()

    def start(self, src, dst):
        self.copies.append(pltpu.make_async_copy(src, dst, self.sems.at[len(self.copies)]))
        self.go()
        return len(self.copies) - 1

    def go(self):
        while self.started < min(len(self.copies), len(self.done) + self.ahead):
            self.copies[self.started].start()
            self.started += 1

    def wait(self, *which):
        for i in which:
            if i not in self.done:
                self.copies[i].wait()
                self.done.add(i)
                self.go()

    def wait_all(self):
        self.wait(*range(len(self.copies)))


def band_rows(rows, slots, off, field, cols, blocks, base, ys, at=0):
    for r, (b, slot) in enumerate(zip(rows, slots)):
        total = None
        for k in range(KB):
            term = dot(blocks[slot, k], field[b + off[k, b] + base, :, 0:cols])
            total = term if total is None else total + term
        ys[r * BK : (r + 1) * BK, at : at + cols] = total.astype(BF16)


def groups_of(nblk):
    inner = list(range(2, nblk - 2))
    return [inner[i : i + 4] for i in range(0, len(inner), 4)]


def project(out, acc, ys, t_v, lo, count):
    size = count * BK
    t = t_v[lo : lo + count].reshape(size, -1)
    for at in range(0, out.shape[0], BK):
        here = slice(at, min(at + BK, out.shape[0]))
        piece = dot(ys[0:size, here], t, ((0,), (0,)))
        out[here, :] = piece if acc is None else acc[here, :] + piece


def columns(z, width):
    return pl.ds(pl.multiple_of(z * width, width), width)


def held(x):
    return pltpu.with_memory_space_constraint(x, pltpu.VMEM)


def edge_kernel(place, z, c, t, intra, inter, tz_inter, sems):
    last = c.shape[0] - 2
    w = c.shape[2]
    zc = intra.shape[2] - w
    loads = Loads(sems)
    near, far = (1 - core_of(place)) * last, core_of(place) * last
    loads.start(c.at[pl.ds(near, 2)], intra.at[:, :, 0:w])
    loads.start(t.at[pl.ds(near, 2), :, columns(z[0], zc)], intra.at[:, :, w : w + zc])
    loads.start(c.at[pl.ds(far, 2)], inter)
    loads.start(t.at[pl.ds(far, 2), :, columns(z[0], zc)], tz_inter)
    loads.wait_all()


def edges(place, z, c, t, zc):
    w = c.shape[2]
    return pl.pallas_call(
        edge_kernel,
        out_shape=(
            jax.ShapeDtypeStruct((2, BK, w + zc), BF16),
            jax.ShapeDtypeStruct((2, BK, w), BF16),
            jax.ShapeDtypeStruct((2, BK, zc), BF16),
        ),
        in_specs=[SMEM, SMEM, ANY, ANY],
        out_specs=(VMEM,) * 3,
        scratch_shapes=[pltpu.SemaphoreType.DMA((4,))],
        compiler_params=params(8),
    )(place, z, stay(c), stay(t))


def lead_of(nblk):
    inner = list(range(2, nblk - 2))
    rest, last = inner[LEAD : len(inner) - LAST], inner[len(inner) - LAST :]
    size = -(-len(rest) // -(-len(rest) // MOST))
    return inner[:LEAD], [rest[i : i + size] for i in range(0, len(rest), size)], last


def first_kernel(
    nblk, z, off, c, t, m, d, p_out, r_out, f, t_v, m_edge, m_v, d_v, ys, yd, sems
):
    w = c.shape[2]
    zc = f.shape[2] - w
    loads = Loads(sems, 8)
    lead, _, _ = lead_of(nblk)
    needs = []
    for g, rows in enumerate(groups_of(nblk)):
        lo, hi = rows[0], rows[-1] + 1
        cuts = [lo, lo + 1, lo + 2, hi] if g == 0 else [lo, lo + 2, hi]
        want = []
        for part in zip(cuts[:-1], cuts[1:]):
            m_id = loads.start(m.at[part[0] : part[1]], m_v.at[part[0] - 2 : part[1] - 2])
            want.append((list(range(*part)), m_id))
        t_id = loads.start(t.at[lo:hi], t_v.at[lo:hi])
        d_ids = ()
        if g == 0:
            near = lead[-1] + 3
            whole = loads.start(c, f.at[:, :, 0:w])
            d_ids = (
                loads.start(d.at[lead[0] : lead[-1] + 1], d_v),
                loads.start(t.at[0:near, :, columns(z[0], zc)], f.at[0:near, :, w : w + zc]),
            )
        needs.append((rows, want, t_id, d_ids))
    for side, at in ((0, 0), (1, nblk - 2)):
        loads.start(m.at[at : at + 2], m_edge.at[2 * side : 2 * side + 2])
        loads.start(t.at[at : at + 2], t_v.at[at : at + 2])
    loads.start(t.at[near:nblk, :, columns(z[0], zc)], f.at[near:nblk, :, w : w + zc])
    for g, (rows, want, t_id, d_ids) in enumerate(needs):
        at = 0
        for part, m_id in want:
            loads.wait(m_id)
            band_rows(
                part, [b - 2 for b in part], off, c, w, m_v, 0,
                ys.at[at * BK : (at + len(part)) * BK],
            )
            at += len(part)
        loads.wait(t_id)
        project(p_out, None if g == 0 else p_out, ys, t_v, rows[0], len(rows))
        if d_ids:
            loads.wait(*d_ids, whole)
            band_rows(lead, range(len(lead)), off, f, w + zc, d_v, 0, yd)
            project(r_out, None, yd, t_v, lead[0], len(lead))
        if g == 1:
            loads.ahead = 64
            loads.go()
    loads.wait_all()


def first(z, off, c, t, m, d, zc):
    nblk, _, w = c.shape
    nt = t.shape[2]
    inner = nblk - 4
    count = len(lead_of(nblk)[0])
    macs = inner * BK * w * (KB * BK + nt) + count * BK * (w + zc) * (KB * BK + nt)
    return pl.pallas_call(
        functools.partial(first_kernel, nblk),
        out_shape=(
            pltpu.VMEM((w, nt), F32),
            pltpu.VMEM((w + zc, nt), F32),
            pltpu.VMEM((nblk, BK, w + zc), BF16),
            pltpu.VMEM((nblk, BK, nt), BF16),
            pltpu.VMEM((4, KB, BK, BK), BF16),
        ),
        in_specs=[SMEM, SMEM, VMEM, ANY, ANY, ANY],
        out_specs=(VMEM,) * 5,
        scratch_shapes=[
            pltpu.VMEM((inner, KB, BK, BK), BF16),
            pltpu.VMEM((count, KB, BK, BK), BF16),
            pltpu.VMEM((4 * BK, w), BF16),
            pltpu.VMEM((count * BK, w + zc), BF16),
            pltpu.SemaphoreType.DMA((5 * len(groups_of(nblk)) + 9,)),
        ],
        compiler_params=params(15),
        cost_estimate=cost(macs, 30 * 2**20),
    )(z, off, held(c), stay(t), stay(m), stay(d))


def middle_kernel(groups, off, after, acc, f, t, d, d_rest, out, d_edge, yd, sems):
    nblk = f.shape[0]
    loads = Loads(sems)
    for side, at in ((0, 0), (1, nblk - 2)):
        loads.start(d.at[at : at + 2], d_edge.at[2 * side : 2 * side + 2])
    for g, rows in enumerate(groups):
        slot = rows[0] - groups[0][0]
        band_rows(rows, range(slot, slot + len(rows)), off, f, f.shape[2], d_rest, 0, yd)
        project(out, acc if g == 0 else out, yd, t, rows[0], len(rows))
    loads.wait_all()


def middle(off, after, acc, f, t, d, d_rest):
    nblk, _, nt = t.shape
    cols = acc.shape[0]
    groups = lead_of(nblk)[1]
    count = sum(map(len, groups))
    return pl.pallas_call(
        functools.partial(middle_kernel, groups),
        out_shape=(pltpu.VMEM((cols, nt), F32), pltpu.VMEM((4, KB, BK, BK), BF16)),
        in_specs=[SMEM, ANY] + [VMEM] * 3 + [ANY, VMEM],
        out_specs=(VMEM, VMEM),
        scratch_shapes=[
            pltpu.VMEM((MOST * BK, cols), BF16),
            pltpu.SemaphoreType.DMA((2,)),
        ],
        compiler_params=params(6),
        cost_estimate=cost(count * BK * cols * (KB * BK + nt), 14 * 2**20),
    )(off, after, held(acc), held(f), held(t), stay(d), held(d_rest))


def boundary_start(nblk, core, f, intra, inter, f_v, sems):
    loads = Loads(sems)
    low = 10 * (1 - core)
    loads.start(f.at[0:4], f_v.at[2:6])
    loads.start(intra, f_v.at[pl.ds(low, 2)])
    loads.start(inter, f_v.at[pl.ds(10 - low, 2)])
    loads.start(f.at[nblk - 4 : nblk], f_v.at[6:10])
    return loads


def boundary_rows(nblk, loads, off, blocks, f_v, ys, at=0):
    cols = f_v.shape[2]
    if loads:
        loads.wait(0, 1, 2)
    band_rows([0, 1], [0, 1], off, f_v, cols, blocks, 2, ys.at[0 : 2 * BK], at)
    if loads:
        loads.wait(3)
    band_rows(
        [nblk - 2, nblk - 1], [2, 3], off, f_v, cols, blocks, 10 - nblk, ys.at[2 * BK : 4 * BK], at
    )


def boundary_sum(acc, ys, t, here, more=()):
    nblk = t.shape[0]
    ends = ((0,), (0,))
    total = acc[here, :]
    for at, rows in ((0, (0, 1)), (2, (nblk - 2, nblk - 1)), (4, more)):
        if rows:
            size = len(rows) * BK
            block = t[rows[0] : rows[-1] + 1].reshape(size, -1)
            total = total + dot(ys[at * BK : at * BK + size, here], block, ends)
    return total


def boundary_kernel(
    nblk, place, off, acc, c, intra, inter, t, m, d,
    send_0, send_1, send_2, send_3, keep, d_rest, f_v, ys, sems, d_sems,
):
    core = core_of(place)
    w = c.shape[2]
    near = boundary_start(nblk, core, c, intra.at[:, :, 0:w], inter, f_v, sems)
    loads = Loads(d_sems)
    _, rest, _ = lead_of(nblk)
    loads.start(d.at[rest[0][0] : nblk - 2], d_rest)
    half = keep.shape[0]
    boundary_rows(nblk, near, off, m, f_v, ys)
    here = pl.ds(pl.multiple_of(core * half, half), half)
    there = pl.ds(pl.multiple_of((1 - core) * half, half), half)
    away = boundary_sum(acc, ys, t, there).astype(BF16)
    for q, send in enumerate((send_0, send_1, send_2, send_3)):
        send[...] = away[q * half // 4 : (q + 1) * half // 4, :]
    keep[...] = boundary_sum(acc, ys, t, here)
    loads.wait_all()


def project_boundary(place, off, acc, c, intra, inter, t, m, d):
    nblk, _, nt = t.shape
    w = acc.shape[0]
    others = nblk - 2 - lead_of(nblk)[1][0][0]
    return pl.pallas_call(
        functools.partial(boundary_kernel, nblk),
        out_shape=(
            *[jax.ShapeDtypeStruct((w // 8, nt), BF16)] * 4,
            jax.ShapeDtypeStruct((w // 2, nt), F32),
            pltpu.VMEM((others, KB, BK, BK), BF16),
            pltpu.VMEM((12, BK, w), BF16),
        ),
        in_specs=[SMEM, SMEM] + [VMEM] * 6 + [ANY],
        out_specs=(VMEM,) * 7,
        scratch_shapes=[
            pltpu.VMEM((4 * BK, w), BF16),
            pltpu.SemaphoreType.DMA((4,)),
            pltpu.SemaphoreType.DMA((1,)),
        ],
        compiler_params=params(10),
        cost_estimate=cost(BK, BK),
    )(place, off, held(acc), held(c), intra, inter, held(t), held(m), stay(d))


def merge_kernel(count, skip, after, a, *refs):
    got, out = refs[:count], refs[count + skip]
    rows = a.shape[0] // count
    for q in range(count):
        here = slice(q * rows, (q + 1) * rows)
        out[here, :] = (a[here, :].astype(F32) + got[q][...].astype(F32)).astype(BF16)


def merge(after, a, got, hold=False, also=()):
    shapes = [jax.ShapeDtypeStruct(a.shape, BF16)]
    if hold:
        shapes.append(jax.ShapeDtypeStruct(after.shape, after.dtype))
    out = pl.pallas_call(
        functools.partial(merge_kernel, len(got), len(also)),
        out_shape=shapes,
        in_specs=[ANY, VMEM] + [VMEM] * len(got) + [ANY] * len(also),
        out_specs=[VMEM, ANY][: len(shapes)],
        input_output_aliases={0: 1} if hold else {},
        compiler_params=params(8),
    )(after, a, *got, *also)
    return out if hold else out[0]


def square_sum(x):
    x = x.astype(F32)
    return jnp.sum(x * x, axis=0, keepdims=True)


def orth_rows(c, t, p):
    return (c.astype(F32) - dot(t, p, ((1,), (1,)))).astype(BF16)


def orth_rows32(c, t, p):
    return c.astype(F32) - dot(t, p, ((1,), (1,)))


def orth_kernel(own, part, place, p, after, x_in, sq_in, c, t, x_out, sq, x_v, out_sems):
    nblk, _, nt = t.shape
    half = p.shape[0]
    core = core_of(place)
    side = core if own else 1 - core
    here = pl.ds(pl.multiple_of(side * half, half), half)
    stores = Loads(out_sems)
    total = None
    for at in range(part[0], part[1], 1):
        block = c[at : at + 1, :, here].reshape(1 * BK, half)
        x = orth_rows32(block, t[at : at + 1].reshape(1 * BK, nt), p[...])
        x_v[at : at + 1] = x.astype(BF16).reshape(1, BK, half)
        squares = square_sum(x)
        total = squares if total is None else total + squares
        stores.start(x_v.at[at : at + 1], x_out.at[at : at + 1, :, here])
    sq[...] = sq_in[...]
    sq[:, here] += total
    stores.wait_all()


def orthogonalize(own, part, place, p, after, x, sq, c, t):
    nblk, _, nt = t.shape
    half = p.shape[0]
    w = 2 * half
    return pl.pallas_call(
        functools.partial(orth_kernel, own, part),
        out_shape=(pltpu.HBM((nblk, BK, w), BF16), jax.ShapeDtypeStruct((1, w), F32)),
        in_specs=[SMEM, VMEM, ANY, ANY, VMEM, VMEM, VMEM],
        out_specs=(ANY, VMEM),
        input_output_aliases={} if x is None else {3: 0},
        scratch_shapes=[
            pltpu.VMEM((nblk, BK, half), BF16),
            pltpu.SemaphoreType.DMA((nblk,)),
        ],
        compiler_params=params(7),
        cost_estimate=cost(nblk * BK * half * nt, 8 * 2**20),
    )(place, p, after, after if x is None else x, sq, held(c), held(t))


def chip_order(bits, side):
    return [(s + side) % bits for s in range(bits)]


def dipole_boundary_kernel(
    nblk, place, off, after, acc, f, near, intra, tz_inter, t, d, d_rest,
    send_0, send_1, keep, f_v, ys, sems,
):
    groups, cols, lanes = keep.shape
    w = near.shape[2]
    bits = groups.bit_length() - 1
    loads = boundary_start(
        nblk, core_of(place), f.at[:, :, w:cols], intra.at[:, :, w:cols], tz_inter, f_v, sems
    )
    _, rest, last = lead_of(nblk)
    slot = last[0] - rest[0][0]
    band_rows(last, range(slot, slot + len(last)), off, f, cols, d_rest, 0, ys.at[4 * BK :])
    boundary_rows(nblk, None, off, d, near, ys)
    boundary_rows(nblk, loads, off, d, f_v, ys, w)
    orders = [chip_order(bits, side) for side in (0, 1)]
    for at in range(0, cols, BK):
        here = slice(at, min(at + BK, cols))
        whole = boundary_sum(acc, ys, t, here, last)
        for g in range(groups):
            owned = []
            for side in (0, 1):
                chip = sum(
                    ((g >> (bits - 1 - s)) & 1) << orders[side][s] for s in range(bits)
                )
                first_lane = (2 * chip + side) * lanes
                owned.append(whole[:, first_lane : first_lane + lanes])
            keep[g, here, :] = jnp.where(core_of(place) == 0, owned[0], owned[1])
            send = (send_0, send_1)[2 * g // groups]
            away = jnp.where(core_of(place) == 0, owned[1], owned[0])
            send[g % (groups // 2), here, :] = away.astype(BF16)


def dipole_boundary(place, off, after, acc, f, near, intra, tz_inter, t, d, d_rest, groups):
    nblk, _, nt = t.shape
    cols = acc.shape[0]
    lanes = nt // (2 * groups)
    return pl.pallas_call(
        functools.partial(dipole_boundary_kernel, nblk),
        out_shape=(
            jax.ShapeDtypeStruct((groups // 2, cols, lanes), BF16),
            jax.ShapeDtypeStruct((groups // 2, cols, lanes), BF16),
            jax.ShapeDtypeStruct((groups, cols, lanes), F32),
        ),
        in_specs=[SMEM, SMEM, ANY] + [VMEM] * 8,
        out_specs=(VMEM,) * 3,
        scratch_shapes=[
            pltpu.VMEM((12, BK, tz_inter.shape[2]), BF16),
            pltpu.VMEM(((4 + LAST) * BK, cols), BF16),
            pltpu.SemaphoreType.DMA((4,)),
        ],
        compiler_params=params(11),
        cost_estimate=cost(4 * BK * cols * (KB * BK + nt), 8 * 2**20),
    )(place, off, after, held(acc), held(f), held(near), intra, tz_inter, held(t), held(d), held(d_rest))


def halve_kernel(step, place, after, keep, *refs):
    got, (send, kept, _) = refs[:-3], refs[-3:]
    half = kept.shape[0]
    orders = [chip_order(step[1], side)[step[0]] for side in (0, 1)]
    which = jnp.where(core_of(place) == 0, orders[0], orders[1])
    bit = jnp.bitwise_and(jnp.right_shift(place[0], which + 1), 1)

    def come(of, g):
        if len(got) == 1:
            return got[0][of * half + g].astype(F32)
        return jnp.where(of == 0, got[0][g], got[1][g]).astype(F32)

    for g in range(half):
        kept[g] = keep[bit * half + g] + come(bit, g)
        send[g] = (keep[(1 - bit) * half + g] + come(1 - bit, g)).astype(BF16)


def halve(step, place, after, keep, got):
    groups, cols, lanes = keep.shape
    half = groups // 2
    return pl.pallas_call(
        functools.partial(halve_kernel, step),
        out_shape=(
            jax.ShapeDtypeStruct((half, cols, lanes), BF16),
            jax.ShapeDtypeStruct((half, cols, lanes), F32),
            jax.ShapeDtypeStruct(after.shape, after.dtype),
        ),
        in_specs=[SMEM, ANY, VMEM] + [VMEM] * len(got),
        out_specs=(VMEM, VMEM, ANY),
        input_output_aliases={1: 2},
        compiler_params=params(8),
    )(place, after, keep, *got)


def settle_kernel(w, after, keep, got, out):
    out[...] = (keep[0, w:, :] + got[0, w:, :].astype(F32)).astype(BF16)


def settle(w, after, keep, got):
    _, cols, lanes = keep.shape
    return pl.pallas_call(
        functools.partial(settle_kernel, w),
        out_shape=jax.ShapeDtypeStruct((cols - w, lanes), BF16),
        in_specs=[ANY, VMEM, VMEM],
        out_specs=VMEM,
        compiler_params=params(8),
    )(after, keep, got)


def stack_kernel(after, *refs):
    out, at = refs[-1], 0
    for piece in refs[:-1]:
        out[at : at + piece.shape[0], :] = piece[...]
        at += piece.shape[0]


def stack(after, pieces):
    rows = sum(piece.shape[0] for piece in pieces)
    return pl.pallas_call(
        stack_kernel,
        out_shape=jax.ShapeDtypeStruct((rows, pieces[0].shape[1]), BF16),
        in_specs=[ANY] + [VMEM] * len(pieces),
        out_specs=VMEM,
        compiler_params=params(8),
    )(after, *pieces)


def finish_kernel(rows, spots, place, z, keep, got, mine, other, sq, *refs):
    pieces, (out, g_v) = refs[:-2], refs[-2:]
    half, w = mine.shape[0], sq.shape[1]
    zc = keep.shape[1] - w
    at = 0
    for piece in pieces:
        for q in range(piece.shape[0] // zc):
            where = pl.multiple_of(jnp.bitwise_xor(z[0], spots[at]) * zc, zc)
            g_v[pl.ds(where, zc), :] = piece[q * zc : (q + 1) * zc, :]
            at += 1
    norm = 1.0 / jnp.sqrt(sq[...] / rows + 1e-06)
    for side in (0, 1):
        here = slice(side * half, (side + 1) * half)
        p = jnp.where(core_of(place) == side, mine[...], other[...])
        raw = keep[0, here, :] + got[0, here, :].astype(F32) - dot(p, g_v[...])
        out[:, here] = (raw.T * norm[:, here]).astype(BF16)


def finish(rows, spots, place, z, keep, got, mine, other, sq, pieces):
    _, cols, lanes = keep.shape
    nt = mine.shape[1]
    w = sq.shape[1]
    return pl.pallas_call(
        functools.partial(finish_kernel, rows, spots),
        out_shape=jax.ShapeDtypeStruct((lanes, w), BF16),
        in_specs=[SMEM, SMEM] + [VMEM] * (5 + len(pieces)),
        out_specs=VMEM,
        scratch_shapes=[pltpu.VMEM((nt, lanes), BF16)],
        compiler_params=params(8),
    )(place, z, keep, got, mine, other, sq, *pieces)


def swap(block, count, mask):
    return lax.ppermute(block, "basis", [(i, i ^ mask[i % 2]) for i in range(count)])


def meet(block, count):
    pairs = [(i, i + 1) for i in range(1, count - 1, 2)]
    return lax.ppermute(block, "basis", pairs + [(b, a) for a, b in pairs])


def exchange(intra, inter, count):
    inter = meet(inter, count)
    return swap(intra, count, (1, 1)), inter


def scalar(x):
    return x.astype(jnp.int32).reshape(1)


def on_device(cont_orbitals, target_orbitals, margin_blocks, dipole_blocks, band_offsets):
    count = lax.axis_size("basis")
    planes = lax.axis_size("orb")
    rows, w = cont_orbitals.shape
    nblk = rows // BK
    nt = target_orbitals.shape[1]
    zc = nt // planes
    chips = count // 2
    bits = chips.bit_length() - 1
    place_s = scalar(lax.axis_index("basis"))
    z = lax.axis_index("orb")
    z_s = scalar(z)
    off = band_offsets.astype(jnp.int32).T
    c = cont_orbitals.reshape(nblk, BK, w)
    t = target_orbitals.reshape(nblk, BK, nt)
    zero = jnp.zeros((1, w), F32)
    both = (1, 1)
    orders = [chip_order(bits, side) for side in (0, 1)]
    masks = [(2 << orders[0][s], 2 << orders[1][s]) for s in range(bits)]

    intra, inter, tz_inter = edges(place_s, z_s, c, t, zc)
    intra, inter = exchange(intra, inter, count)
    tz_inter = meet(tz_inter, count)
    p_acc, r_acc, f, t_v, m_edge = first(z_s, off, c, t, margin_blocks, dipole_blocks, zc)
    *sends, keep, d_rest, near = project_boundary(
        place_s, off, p_acc, c, intra, inter, t_v, m_edge, dipole_blocks
    )
    got = [swap(send, count, both) for send in sends]
    part, r_acc = merge(r_acc, keep, got, hold=True, also=(tz_inter,))

    for s in range(bits):
        got = [swap(part, count, masks[s])]
        if s == 0:
            r_acc, d_edge = middle(off, part, r_acc, f, t_v, dipole_blocks, d_rest)
            part, r_acc = merge(r_acc, part, got, hold=True)
            continue
        if s == 1:
            *sends, keep = dipole_boundary(
                place_s, off, part, r_acc, f, near, intra, tz_inter, t_v, d_edge, d_rest, chips
            )
            got_r = [swap(send, count, both) for send in sends]
            send = sends[0]
        else:
            send, keep, part = halve((s - 2, bits), place_s, part, keep, got_r)
            got_r = [swap(send, count, masks[s - 2])]
        part = merge(send, part, got)
    send, keep, part = halve((bits - 2, bits), place_s, part, keep, got_r)
    got_r = [swap(send, count, masks[bits - 2])]
    other = swap(part, count, both)

    x, sq = orthogonalize(True, (0, nblk), place_s, part, part, None, zero, c, t_v)
    x, sq = orthogonalize(False, (0, nblk), place_s, other, part, x, sq, c, t_v)
    send, keep, sq = halve((bits - 1, bits), place_s, sq, keep, got_r)
    got_r = [swap(send, count, masks[bits - 1])]
    tail = [both] + masks
    sq = sq + swap(sq, count, tail.pop(0))
    sq = sq + swap(sq, count, tail.pop(0))
    pieces = [settle(w, sq, keep, got_r[0])]
    spots, step = [0], planes // 2
    while step:
        whole = pieces[0]
        if len(pieces) > 1:
            whole = stack(sq, pieces)
        pieces.append(lax.ppermute(whole, "orb", [(i, i ^ step) for i in range(planes)]))
        spots += [spot ^ step for spot in spots]
        step //= 2
    for mask in tail:
        sq = sq + swap(sq, count, mask)
    dipole_mo = finish(rows * count, spots, place_s, z_s, keep, got_r[0], part, other, sq, pieces)
    return (x.reshape(rows, w), dipole_mo)


def solution(mesh):
    return jax.shard_map(
        on_device,
        mesh=mesh,
        in_specs=(
            P("basis", "orb"),
            P("basis", None),
            P("basis", None, None, None),
            P("basis", None, None, None),
            P("basis", None),
        ),
        out_specs=(P("basis", "orb"), P("basis", "orb")),
        check_vma=False,
    )
```

```python
import functools

import jax
import jax.numpy as jnp
from jax import lax
from jax.experimental import pallas as pl
from jax.experimental.pallas import tpu as pltpu
from jax.sharding import PartitionSpec as P

BK = 256
KB = 4
LEAD = 1
LAST = 2
MOST = 5
F32 = jnp.float32
BF16 = jnp.bfloat16
ANY = pl.BlockSpec(memory_space=pl.ANY)
VMEM = pl.BlockSpec(memory_space=pltpu.VMEM)
SMEM = pl.BlockSpec(memory_space=pltpu.SMEM)


def core_of(place):
    return jnp.bitwise_and(place[0], 1)


def stay(x):
    return pltpu.with_memory_space_constraint(x, pltpu.HBM)


def params(mib=40):
    return pltpu.CompilerParams(vmem_limit_bytes=mib * 2**20)


def cost(macs, data):
    return pl.CostEstimate(flops=2 * macs, bytes_accessed=data, transcendentals=0)


def dot(a, b, dims=((1,), (0,))):
    return lax.dot_general(a, b, (dims, ((), ())), preferred_element_type=F32)


class Loads:
    def __init__(self, sems, ahead=64):
        self.sems, self.ahead = sems, ahead
        self.copies, self.started, self.done = [], 0, set()

    def start(self, src, dst):
        self.copies.append(pltpu.make_async_copy(src, dst, self.sems.at[len(self.copies)]))
        self.go()
        return len(self.copies) - 1

    def go(self):
        while self.started < min(len(self.copies), len(self.done) + self.ahead):
            self.copies[self.started].start()
            self.started += 1

    def wait(self, *which):
        for i in which:
            if i not in self.done:
                self.copies[i].wait()
                self.done.add(i)
                self.go()

    def wait_all(self):
        self.wait(*range(len(self.copies)))


def band_rows(rows, slots, off, field, cols, blocks, base, ys, at=0):
    for r, (b, slot) in enumerate(zip(rows, slots)):
        total = None
        for k in range(KB):
            term = dot(blocks[slot, k], field[b + off[k, b] + base, :, 0:cols])
            total = term if total is None else total + term
        ys[r * BK : (r + 1) * BK, at : at + cols] = total.astype(BF16)


def groups_of(nblk):
    inner = list(range(2, nblk - 2))
    return [inner[i : i + 4] for i in range(0, len(inner), 4)]


def project(out, acc, ys, t_v, lo, count):
    size = count * BK
    t = t_v[lo : lo + count].reshape(size, -1)
    for at in range(0, out.shape[0], BK):
        here = slice(at, min(at + BK, out.shape[0]))
        piece = dot(ys[0:size, here], t, ((0,), (0,)))
        out[here, :] = piece if acc is None else acc[here, :] + piece


def columns(z, width):
    return pl.ds(pl.multiple_of(z * width, width), width)


def held(x):
    return pltpu.with_memory_space_constraint(x, pltpu.VMEM)


def edge_kernel(place, z, c, t, intra, inter, tz_inter, sems):
    last = c.shape[0] - 2
    w = c.shape[2]
    zc = intra.shape[2] - w
    loads = Loads(sems)
    near, far = (1 - core_of(place)) * last, core_of(place) * last
    loads.start(c.at[pl.ds(near, 2)], intra.at[:, :, 0:w])
    loads.start(t.at[pl.ds(near, 2), :, columns(z[0], zc)], intra.at[:, :, w : w + zc])
    loads.start(c.at[pl.ds(far, 2)], inter)
    loads.start(t.at[pl.ds(far, 2), :, columns(z[0], zc)], tz_inter)
    loads.wait_all()


def edges(place, z, c, t, zc):
    w = c.shape[2]
    return pl.pallas_call(
        edge_kernel,
        out_shape=(
            jax.ShapeDtypeStruct((2, BK, w + zc), BF16),
            jax.ShapeDtypeStruct((2, BK, w), BF16),
            jax.ShapeDtypeStruct((2, BK, zc), BF16),
        ),
        in_specs=[SMEM, SMEM, ANY, ANY],
        out_specs=(VMEM,) * 3,
        scratch_shapes=[pltpu.SemaphoreType.DMA((4,))],
        compiler_params=params(8),
    )(place, z, stay(c), stay(t))


def lead_of(nblk):
    inner = list(range(2, nblk - 2))
    rest, last = inner[LEAD : len(inner) - LAST], inner[len(inner) - LAST :]
    size = -(-len(rest) // -(-len(rest) // MOST))
    return inner[:LEAD], [rest[i : i + size] for i in range(0, len(rest), size)], last


def first_kernel(
    nblk, z, off, c, t, m, d, p_out, r_out, f, t_v, m_edge, m_v, d_v, ys, yd, sems
):
    w = c.shape[2]
    zc = f.shape[2] - w
    loads = Loads(sems, 8)
    lead, _, _ = lead_of(nblk)
    needs = []
    for g, rows in enumerate(groups_of(nblk)):
        lo, hi = rows[0], rows[-1] + 1
        cuts = [lo, lo + 1, lo + 2, hi] if g == 0 else [lo, lo + 2, hi]
        want = []
        for part in zip(cuts[:-1], cuts[1:]):
            m_id = loads.start(m.at[part[0] : part[1]], m_v.at[part[0] - 2 : part[1] - 2])
            want.append((list(range(*part)), m_id))
        t_id = loads.start(t.at[lo:hi], t_v.at[lo:hi])
        d_ids = ()
        if g == 0:
            near = lead[-1] + 3
            whole = loads.start(c, f.at[:, :, 0:w])
            d_ids = (
                loads.start(d.at[lead[0] : lead[-1] + 1], d_v),
                loads.start(t.at[0:near, :, columns(z[0], zc)], f.at[0:near, :, w : w + zc]),
            )
        needs.append((rows, want, t_id, d_ids))
    for side, at in ((0, 0), (1, nblk - 2)):
        loads.start(m.at[at : at + 2], m_edge.at[2 * side : 2 * side + 2])
        loads.start(t.at[at : at + 2], t_v.at[at : at + 2])
    loads.start(t.at[near:nblk, :, columns(z[0], zc)], f.at[near:nblk, :, w : w + zc])
    for g, (rows, want, t_id, d_ids) in enumerate(needs):
        at = 0
        for part, m_id in want:
            loads.wait(m_id)
            band_rows(
                part, [b - 2 for b in part], off, c, w, m_v, 0,
                ys.at[at * BK : (at + len(part)) * BK],
            )
            at += len(part)
        loads.wait(t_id)
        project(p_out, None if g == 0 else p_out, ys, t_v, rows[0], len(rows))
        if d_ids:
            loads.wait(*d_ids, whole)
            band_rows(lead, range(len(lead)), off, f, w + zc, d_v, 0, yd)
            project(r_out, None, yd, t_v, lead[0], len(lead))
        if g == 1:
            loads.ahead = 64
            loads.go()
    loads.wait_all()


def first(z, off, c, t, m, d, zc):
    nblk, _, w = c.shape
    nt = t.shape[2]
    inner = nblk - 4
    count = len(lead_of(nblk)[0])
    macs = inner * BK * w * (KB * BK + nt) + count * BK * (w + zc) * (KB * BK + nt)
    return pl.pallas_call(
        functools.partial(first_kernel, nblk),
        out_shape=(
            pltpu.VMEM((w, nt), F32),
            pltpu.VMEM((w + zc, nt), F32),
            pltpu.VMEM((nblk, BK, w + zc), BF16),
            pltpu.VMEM((nblk, BK, nt), BF16),
            pltpu.VMEM((4, KB, BK, BK), BF16),
        ),
        in_specs=[SMEM, SMEM, VMEM, ANY, ANY, ANY],
        out_specs=(VMEM,) * 5,
        scratch_shapes=[
            pltpu.VMEM((inner, KB, BK, BK), BF16),
            pltpu.VMEM((count, KB, BK, BK), BF16),
            pltpu.VMEM((4 * BK, w), BF16),
            pltpu.VMEM((count * BK, w + zc), BF16),
            pltpu.SemaphoreType.DMA((5 * len(groups_of(nblk)) + 9,)),
        ],
        compiler_params=params(15),
        cost_estimate=cost(macs, 30 * 2**20),
    )(z, off, held(c), stay(t), stay(m), stay(d))


def middle_kernel(groups, off, after, acc, f, t, d, d_rest, out, d_edge, yd, sems):
    nblk = f.shape[0]
    loads = Loads(sems)
    for side, at in ((0, 0), (1, nblk - 2)):
        loads.start(d.at[at : at + 2], d_edge.at[2 * side : 2 * side + 2])
    for g, rows in enumerate(groups):
        slot = rows[0] - groups[0][0]
        band_rows(rows, range(slot, slot + len(rows)), off, f, f.shape[2], d_rest, 0, yd)
        project(out, acc if g == 0 else out, yd, t, rows[0], len(rows))
    loads.wait_all()


def middle(off, after, acc, f, t, d, d_rest):
    nblk, _, nt = t.shape
    cols = acc.shape[0]
    groups = lead_of(nblk)[1]
    count = sum(map(len, groups))
    return pl.pallas_call(
        functools.partial(middle_kernel, groups),
        out_shape=(pltpu.VMEM((cols, nt), F32), pltpu.VMEM((4, KB, BK, BK), BF16)),
        in_specs=[SMEM, ANY] + [VMEM] * 3 + [ANY, VMEM],
        out_specs=(VMEM, VMEM),
        scratch_shapes=[
            pltpu.VMEM((MOST * BK, cols), BF16),
            pltpu.SemaphoreType.DMA((2,)),
        ],
        compiler_params=params(6),
        cost_estimate=cost(count * BK * cols * (KB * BK + nt), 14 * 2**20),
    )(off, after, held(acc), held(f), held(t), stay(d), held(d_rest))


def boundary_start(nblk, core, f, intra, inter, f_v, sems):
    loads = Loads(sems)
    low = 10 * (1 - core)
    loads.start(f.at[0:4], f_v.at[2:6])
    loads.start(intra, f_v.at[pl.ds(low, 2)])
    loads.start(inter, f_v.at[pl.ds(10 - low, 2)])
    loads.start(f.at[nblk - 4 : nblk], f_v.at[6:10])
    return loads


def boundary_rows(nblk, loads, off, blocks, f_v, ys, at=0):
    cols = f_v.shape[2]
    if loads:
        loads.wait(0, 1, 2)
    band_rows([0, 1], [0, 1], off, f_v, cols, blocks, 2, ys.at[0 : 2 * BK], at)
    if loads:
        loads.wait(3)
    band_rows(
        [nblk - 2, nblk - 1], [2, 3], off, f_v, cols, blocks, 10 - nblk, ys.at[2 * BK : 4 * BK], at
    )


def boundary_sum(acc, ys, t, here, more=()):
    nblk = t.shape[0]
    ends = ((0,), (0,))
    total = acc[here, :]
    for at, rows in ((0, (0, 1)), (2, (nblk - 2, nblk - 1)), (4, more)):
        if rows:
            size = len(rows) * BK
            block = t[rows[0] : rows[-1] + 1].reshape(size, -1)
            total = total + dot(ys[at * BK : at * BK + size, here], block, ends)
    return total


def boundary_kernel(
    nblk, place, off, acc, c, intra, inter, t, m, d,
    send_0, send_1, keep, d_rest, f_v, ys, sems, d_sems,
):
    core = core_of(place)
    w = c.shape[2]
    near = boundary_start(nblk, core, c, intra.at[:, :, 0:w], inter, f_v, sems)
    loads = Loads(d_sems)
    _, rest, _ = lead_of(nblk)
    loads.start(d.at[rest[0][0] : nblk - 2], d_rest)
    half = keep.shape[0]
    boundary_rows(nblk, near, off, m, f_v, ys)
    here = pl.ds(pl.multiple_of(core * half, half), half)
    there = pl.ds(pl.multiple_of((1 - core) * half, half), half)
    away = boundary_sum(acc, ys, t, there).astype(BF16)
    for q, send in enumerate((send_0, send_1)):
        send[...] = away[q * half // 2 : (q + 1) * half // 2, :]
    keep[...] = boundary_sum(acc, ys, t, here)
    loads.wait_all()


def project_boundary(place, off, acc, c, intra, inter, t, m, d):
    nblk, _, nt = t.shape
    w = acc.shape[0]
    others = nblk - 2 - lead_of(nblk)[1][0][0]
    return pl.pallas_call(
        functools.partial(boundary_kernel, nblk),
        out_shape=(
            *[jax.ShapeDtypeStruct((w // 4, nt), BF16)] * 2,
            jax.ShapeDtypeStruct((w // 2, nt), F32),
            pltpu.VMEM((others, KB, BK, BK), BF16),
            pltpu.VMEM((12, BK, w), BF16),
        ),
        in_specs=[SMEM, SMEM] + [VMEM] * 6 + [ANY],
        out_specs=(VMEM,) * 5,
        scratch_shapes=[
            pltpu.VMEM((4 * BK, w), BF16),
            pltpu.SemaphoreType.DMA((4,)),
            pltpu.SemaphoreType.DMA((1,)),
        ],
        compiler_params=params(10),
        cost_estimate=cost(BK, BK),
    )(place, off, held(acc), held(c), intra, inter, held(t), held(m), stay(d))


def merge_kernel(count, skip, after, a, *refs):
    got, out = refs[:count], refs[count + skip]
    rows = a.shape[0] // count
    for q in range(count):
        here = slice(q * rows, (q + 1) * rows)
        out[here, :] = (a[here, :].astype(F32) + got[q][...].astype(F32)).astype(BF16)


def merge(after, a, got, hold=False, also=()):
    shapes = [jax.ShapeDtypeStruct(a.shape, BF16)]
    if hold:
        shapes.append(jax.ShapeDtypeStruct(after.shape, after.dtype))
    out = pl.pallas_call(
        functools.partial(merge_kernel, len(got), len(also)),
        out_shape=shapes,
        in_specs=[ANY, VMEM] + [VMEM] * len(got) + [ANY] * len(also),
        out_specs=[VMEM, ANY][: len(shapes)],
        input_output_aliases={0: 1} if hold else {},
        compiler_params=params(8),
    )(after, a, *got, *also)
    return out if hold else out[0]


def square_sum(x):
    x = x.astype(F32)
    return jnp.sum(x * x, axis=0, keepdims=True)


def orth_rows(c, t, p):
    return (c.astype(F32) - dot(t, p, ((1,), (1,)))).astype(BF16)


def orth_rows32(c, t, p):
    return c.astype(F32) - dot(t, p, ((1,), (1,)))


def orth_kernel(own, part, place, p, after, x_in, sq_in, c, t, x_out, sq, x_v, out_sems):
    nblk, _, nt = t.shape
    half = p.shape[0]
    core = core_of(place)
    side = core if own else 1 - core
    here = pl.ds(pl.multiple_of(side * half, half), half)
    stores = Loads(out_sems)
    total = None
    for at in range(part[0], part[1], 1):
        block = c[at : at + 1, :, here].reshape(1 * BK, half)
        x = orth_rows32(block, t[at : at + 1].reshape(1 * BK, nt), p[...])
        x_v[at : at + 1] = x.astype(BF16).reshape(1, BK, half)
        squares = square_sum(x)
        total = squares if total is None else total + squares
        stores.start(x_v.at[at : at + 1], x_out.at[at : at + 1, :, here])
    sq[...] = sq_in[...]
    sq[:, here] += total
    stores.wait_all()


def orthogonalize(own, part, place, p, after, x, sq, c, t):
    nblk, _, nt = t.shape
    half = p.shape[0]
    w = 2 * half
    return pl.pallas_call(
        functools.partial(orth_kernel, own, part),
        out_shape=(pltpu.HBM((nblk, BK, w), BF16), jax.ShapeDtypeStruct((1, w), F32)),
        in_specs=[SMEM, VMEM, ANY, ANY, VMEM, VMEM, VMEM],
        out_specs=(ANY, VMEM),
        input_output_aliases={} if x is None else {3: 0},
        scratch_shapes=[
            pltpu.VMEM((nblk, BK, half), BF16),
            pltpu.SemaphoreType.DMA((nblk,)),
        ],
        compiler_params=params(7),
        cost_estimate=cost(nblk * BK * half * nt, 8 * 2**20),
    )(place, p, after, after if x is None else x, sq, held(c), held(t))


def chip_order(bits, side):
    return [(s + side) % bits for s in range(bits)]


def dipole_boundary_kernel(
    nblk, place, off, after, acc, f, near, intra, tz_inter, t, d, d_rest,
    send_0, send_1, keep, f_v, ys, sems,
):
    groups, cols, lanes = keep.shape
    w = near.shape[2]
    bits = groups.bit_length() - 1
    loads = boundary_start(
        nblk, core_of(place), f.at[:, :, w:cols], intra.at[:, :, w:cols], tz_inter, f_v, sems
    )
    _, rest, last = lead_of(nblk)
    slot = last[0] - rest[0][0]
    band_rows(last, range(slot, slot + len(last)), off, f, cols, d_rest, 0, ys.at[4 * BK :])
    boundary_rows(nblk, None, off, d, near, ys)
    boundary_rows(nblk, loads, off, d, f_v, ys, w)
    orders = [chip_order(bits, side) for side in (0, 1)]
    for at in range(0, cols, BK):
        here = slice(at, min(at + BK, cols))
        whole = boundary_sum(acc, ys, t, here, last)
        for g in range(groups):
            owned = []
            for side in (0, 1):
                chip = sum(
                    ((g >> (bits - 1 - s)) & 1) << orders[side][s] for s in range(bits)
                )
                first_lane = (2 * chip + side) * lanes
                owned.append(whole[:, first_lane : first_lane + lanes])
            keep[g, here, :] = jnp.where(core_of(place) == 0, owned[0], owned[1])
            send = (send_0, send_1)[2 * g // groups]
            away = jnp.where(core_of(place) == 0, owned[1], owned[0])
            send[g % (groups // 2), here, :] = away.astype(BF16)


def dipole_boundary(place, off, after, acc, f, near, intra, tz_inter, t, d, d_rest, groups):
    nblk, _, nt = t.shape
    cols = acc.shape[0]
    lanes = nt // (2 * groups)
    return pl.pallas_call(
        functools.partial(dipole_boundary_kernel, nblk),
        out_shape=(
            jax.ShapeDtypeStruct((groups // 2, cols, lanes), BF16),
            jax.ShapeDtypeStruct((groups // 2, cols, lanes), BF16),
            jax.ShapeDtypeStruct((groups, cols, lanes), F32),
        ),
        in_specs=[SMEM, SMEM, ANY] + [VMEM] * 8,
        out_specs=(VMEM,) * 3,
        scratch_shapes=[
            pltpu.VMEM((12, BK, tz_inter.shape[2]), BF16),
            pltpu.VMEM(((4 + LAST) * BK, cols), BF16),
            pltpu.SemaphoreType.DMA((4,)),
        ],
        compiler_params=params(11),
        cost_estimate=cost(4 * BK * cols * (KB * BK + nt), 8 * 2**20),
    )(place, off, after, held(acc), held(f), held(near), intra, tz_inter, held(t), held(d), held(d_rest))


def halve_kernel(step, place, after, keep, *refs):
    got, (send, kept, _) = refs[:-3], refs[-3:]
    half = kept.shape[0]
    orders = [chip_order(step[1], side)[step[0]] for side in (0, 1)]
    which = jnp.where(core_of(place) == 0, orders[0], orders[1])
    bit = jnp.bitwise_and(jnp.right_shift(place[0], which + 1), 1)

    def come(of, g):
        if len(got) == 1:
            return got[0][of * half + g].astype(F32)
        return jnp.where(of == 0, got[0][g], got[1][g]).astype(F32)

    for g in range(half):
        kept[g] = keep[bit * half + g] + come(bit, g)
        send[g] = (keep[(1 - bit) * half + g] + come(1 - bit, g)).astype(BF16)


def halve(step, place, after, keep, got):
    groups, cols, lanes = keep.shape
    half = groups // 2
    return pl.pallas_call(
        functools.partial(halve_kernel, step),
        out_shape=(
            jax.ShapeDtypeStruct((half, cols, lanes), BF16),
            jax.ShapeDtypeStruct((half, cols, lanes), F32),
            jax.ShapeDtypeStruct(after.shape, after.dtype),
        ),
        in_specs=[SMEM, ANY, VMEM] + [VMEM] * len(got),
        out_specs=(VMEM, VMEM, ANY),
        input_output_aliases={1: 2},
        compiler_params=params(8),
    )(place, after, keep, *got)


def settle_kernel(w, after, keep, got, out):
    out[...] = (keep[0, w:, :] + got[0, w:, :].astype(F32)).astype(BF16)


def settle(w, after, keep, got):
    _, cols, lanes = keep.shape
    return pl.pallas_call(
        functools.partial(settle_kernel, w),
        out_shape=jax.ShapeDtypeStruct((cols - w, lanes), BF16),
        in_specs=[ANY, VMEM, VMEM],
        out_specs=VMEM,
        compiler_params=params(8),
    )(after, keep, got)


def stack_kernel(after, *refs):
    out, at = refs[-1], 0
    for piece in refs[:-1]:
        out[at : at + piece.shape[0], :] = piece[...]
        at += piece.shape[0]


def stack(after, pieces):
    rows = sum(piece.shape[0] for piece in pieces)
    return pl.pallas_call(
        stack_kernel,
        out_shape=jax.ShapeDtypeStruct((rows, pieces[0].shape[1]), BF16),
        in_specs=[ANY] + [VMEM] * len(pieces),
        out_specs=VMEM,
        compiler_params=params(8),
    )(after, *pieces)


def finish_kernel(rows, spots, place, z, keep, got, mine, other, sq, *refs):
    pieces, (out, g_v) = refs[:-2], refs[-2:]
    half, w = mine.shape[0], sq.shape[1]
    zc = keep.shape[1] - w
    at = 0
    for piece in pieces:
        for q in range(piece.shape[0] // zc):
            where = pl.multiple_of(jnp.bitwise_xor(z[0], spots[at]) * zc, zc)
            g_v[pl.ds(where, zc), :] = piece[q * zc : (q + 1) * zc, :]
            at += 1
    norm = 1.0 / jnp.sqrt(sq[...] / rows + 1e-06)
    for side in (0, 1):
        here = slice(side * half, (side + 1) * half)
        p = jnp.where(core_of(place) == side, mine[...], other[...])
        raw = keep[0, here, :] + got[0, here, :].astype(F32) - dot(p, g_v[...])
        out[:, here] = (raw.T * norm[:, here]).astype(BF16)


def finish(rows, spots, place, z, keep, got, mine, other, sq, pieces):
    _, cols, lanes = keep.shape
    nt = mine.shape[1]
    w = sq.shape[1]
    return pl.pallas_call(
        functools.partial(finish_kernel, rows, spots),
        out_shape=jax.ShapeDtypeStruct((lanes, w), BF16),
        in_specs=[SMEM, SMEM] + [VMEM] * (5 + len(pieces)),
        out_specs=VMEM,
        scratch_shapes=[pltpu.VMEM((nt, lanes), BF16)],
        compiler_params=params(8),
    )(place, z, keep, got, mine, other, sq, *pieces)


def swap(block, count, mask):
    return lax.ppermute(block, "basis", [(i, i ^ mask[i % 2]) for i in range(count)])


def meet(block, count):
    pairs = [(i, i + 1) for i in range(1, count - 1, 2)]
    return lax.ppermute(block, "basis", pairs + [(b, a) for a, b in pairs])


def exchange(intra, inter, count):
    inter = meet(inter, count)
    return swap(intra, count, (1, 1)), inter


def scalar(x):
    return x.astype(jnp.int32).reshape(1)


def on_device(cont_orbitals, target_orbitals, margin_blocks, dipole_blocks, band_offsets):
    count = lax.axis_size("basis")
    planes = lax.axis_size("orb")
    rows, w = cont_orbitals.shape
    nblk = rows // BK
    nt = target_orbitals.shape[1]
    zc = nt // planes
    chips = count // 2
    bits = chips.bit_length() - 1
    place_s = scalar(lax.axis_index("basis"))
    z = lax.axis_index("orb")
    z_s = scalar(z)
    off = band_offsets.astype(jnp.int32).T
    c = cont_orbitals.reshape(nblk, BK, w)
    t = target_orbitals.reshape(nblk, BK, nt)
    zero = jnp.zeros((1, w), F32)
    both = (1, 1)
    orders = [chip_order(bits, side) for side in (0, 1)]
    masks = [(2 << orders[0][s], 2 << orders[1][s]) for s in range(bits)]

    intra, inter, tz_inter = edges(place_s, z_s, c, t, zc)
    intra, inter = exchange(intra, inter, count)
    tz_inter = meet(tz_inter, count)
    p_acc, r_acc, f, t_v, m_edge = first(z_s, off, c, t, margin_blocks, dipole_blocks, zc)
    *sends, keep, d_rest, near = project_boundary(
        place_s, off, p_acc, c, intra, inter, t_v, m_edge, dipole_blocks
    )
    got = [swap(send, count, both) for send in sends]
    part, r_acc = merge(r_acc, keep, got, hold=True, also=(tz_inter,))

    for s in range(bits):
        got = [swap(part, count, masks[s])]
        if s == 0:
            r_acc, d_edge = middle(off, part, r_acc, f, t_v, dipole_blocks, d_rest)
            part, r_acc = merge(r_acc, part, got, hold=True)
            continue
        if s == 1:
            *sends, keep = dipole_boundary(
                place_s, off, part, r_acc, f, near, intra, tz_inter, t_v, d_edge, d_rest, chips
            )
            got_r = [swap(send, count, both) for send in sends]
            send = sends[0]
        else:
            send, keep, part = halve((s - 2, bits), place_s, part, keep, got_r)
            got_r = [swap(send, count, masks[s - 2])]
        part = merge(send, part, got)
    send, keep, part = halve((bits - 2, bits), place_s, part, keep, got_r)
    got_r = [swap(send, count, masks[bits - 2])]
    other = swap(part, count, both)

    x, sq = orthogonalize(True, (0, nblk), place_s, part, part, None, zero, c, t_v)
    x, sq = orthogonalize(False, (0, nblk), place_s, other, part, x, sq, c, t_v)
    send, keep, sq = halve((bits - 1, bits), place_s, sq, keep, got_r)
    got_r = [swap(send, count, masks[bits - 1])]
    tail = [both] + masks
    sq = sq + swap(sq, count, tail.pop(0))
    sq = sq + swap(sq, count, tail.pop(0))
    pieces = [settle(w, sq, keep, got_r[0])]
    spots, step = [0], planes // 2
    while step:
        whole = pieces[0]
        if len(pieces) > 1:
            whole = stack(sq, pieces)
        pieces.append(lax.ppermute(whole, "orb", [(i, i ^ step) for i in range(planes)]))
        spots += [spot ^ step for spot in spots]
        step //= 2
    for mask in tail:
        sq = sq + swap(sq, count, mask)
    dipole_mo = finish(rows * count, spots, place_s, z_s, keep, got_r[0], part, other, sq, pieces)
    return (x.reshape(rows, w), dipole_mo)


def solution(mesh):
    return jax.shard_map(
        on_device,
        mesh=mesh,
        in_specs=(
            P("basis", "orb"),
            P("basis", None),
            P("basis", None, None, None),
            P("basis", None, None, None),
            P("basis", None),
        ),
        out_specs=(P("basis", "orb"), P("basis", "orb")),
        check_vma=False,
    )
```

```python
import functools

import jax
import jax.numpy as jnp
from jax import lax
from jax.experimental import pallas as pl
from jax.experimental.pallas import tpu as pltpu
from jax.sharding import PartitionSpec as P

BK = 256
KB = 4
LEAD = 1
LAST = 2
MOST = 5
F32 = jnp.float32
BF16 = jnp.bfloat16
ANY = pl.BlockSpec(memory_space=pl.ANY)
VMEM = pl.BlockSpec(memory_space=pltpu.VMEM)
SMEM = pl.BlockSpec(memory_space=pltpu.SMEM)


def core_of(place):
    return jnp.bitwise_and(place[0], 1)


def stay(x):
    return pltpu.with_memory_space_constraint(x, pltpu.HBM)


def params(mib=40):
    return pltpu.CompilerParams(vmem_limit_bytes=mib * 2**20)


def cost(macs, data):
    return pl.CostEstimate(flops=2 * macs, bytes_accessed=data, transcendentals=0)


def dot(a, b, dims=((1,), (0,))):
    return lax.dot_general(a, b, (dims, ((), ())), preferred_element_type=F32)


class Loads:
    def __init__(self, sems, ahead=64):
        self.sems, self.ahead = sems, ahead
        self.copies, self.started, self.done = [], 0, set()

    def start(self, src, dst):
        self.copies.append(pltpu.make_async_copy(src, dst, self.sems.at[len(self.copies)]))
        self.go()
        return len(self.copies) - 1

    def go(self):
        while self.started < min(len(self.copies), len(self.done) + self.ahead):
            self.copies[self.started].start()
            self.started += 1

    def wait(self, *which):
        for i in which:
            if i not in self.done:
                self.copies[i].wait()
                self.done.add(i)
                self.go()

    def wait_all(self):
        self.wait(*range(len(self.copies)))


def band_rows(rows, slots, off, field, cols, blocks, base, ys, at=0):
    for r, (b, slot) in enumerate(zip(rows, slots)):
        total = None
        for k in range(KB):
            term = dot(blocks[slot, k], field[b + off[k, b] + base, :, 0:cols])
            total = term if total is None else total + term
        ys[r * BK : (r + 1) * BK, at : at + cols] = total.astype(BF16)


def groups_of(nblk):
    inner = list(range(2, nblk - 2))
    return [inner[i : i + 4] for i in range(0, len(inner), 4)]


def project(out, acc, ys, t_v, lo, count):
    size = count * BK
    t = t_v[lo : lo + count].reshape(size, -1)
    for at in range(0, out.shape[0], BK):
        here = slice(at, min(at + BK, out.shape[0]))
        piece = dot(ys[0:size, here], t, ((0,), (0,)))
        out[here, :] = piece if acc is None else acc[here, :] + piece


def columns(z, width):
    return pl.ds(pl.multiple_of(z * width, width), width)


def held(x):
    return pltpu.with_memory_space_constraint(x, pltpu.VMEM)


def edge_kernel(place, z, c, t, intra, inter, tz_inter, sems):
    last = c.shape[0] - 2
    w = c.shape[2]
    zc = intra.shape[2] - w
    loads = Loads(sems)
    near, far = (1 - core_of(place)) * last, core_of(place) * last
    loads.start(c.at[pl.ds(near, 2)], intra.at[:, :, 0:w])
    loads.start(t.at[pl.ds(near, 2), :, columns(z[0], zc)], intra.at[:, :, w : w + zc])
    loads.start(c.at[pl.ds(far, 2)], inter)
    loads.start(t.at[pl.ds(far, 2), :, columns(z[0], zc)], tz_inter)
    loads.wait_all()


def edges(place, z, c, t, zc):
    w = c.shape[2]
    return pl.pallas_call(
        edge_kernel,
        out_shape=(
            jax.ShapeDtypeStruct((2, BK, w + zc), BF16),
            jax.ShapeDtypeStruct((2, BK, w), BF16),
            jax.ShapeDtypeStruct((2, BK, zc), BF16),
        ),
        in_specs=[SMEM, SMEM, ANY, ANY],
        out_specs=(VMEM,) * 3,
        scratch_shapes=[pltpu.SemaphoreType.DMA((4,))],
        compiler_params=params(8),
    )(place, z, stay(c), stay(t))


def lead_of(nblk):
    inner = list(range(2, nblk - 2))
    rest, last = inner[LEAD : len(inner) - LAST], inner[len(inner) - LAST :]
    size = -(-len(rest) // -(-len(rest) // MOST))
    return inner[:LEAD], [rest[i : i + size] for i in range(0, len(rest), size)], last


def first_kernel(
    nblk, z, off, c, t, m, d, p_out, r_out, f, t_v, m_edge, m_v, d_v, ys, yd, sems
):
    w = c.shape[2]
    zc = f.shape[2] - w
    loads = Loads(sems, 8)
    lead, _, _ = lead_of(nblk)
    needs = []
    for g, rows in enumerate(groups_of(nblk)):
        lo, hi = rows[0], rows[-1] + 1
        cuts = [lo, lo + 1, lo + 2, hi] if g == 0 else [lo, lo + 2, hi]
        want = []
        for part in zip(cuts[:-1], cuts[1:]):
            m_id = loads.start(m.at[part[0] : part[1]], m_v.at[part[0] - 2 : part[1] - 2])
            want.append((list(range(*part)), m_id))
        t_id = loads.start(t.at[lo:hi], t_v.at[lo:hi])
        d_ids = ()
        if g == 0:
            near = lead[-1] + 3
            whole = loads.start(c, f.at[:, :, 0:w])
            d_ids = (
                loads.start(d.at[lead[0] : lead[-1] + 1], d_v),
                loads.start(t.at[0:near, :, columns(z[0], zc)], f.at[0:near, :, w : w + zc]),
            )
        needs.append((rows, want, t_id, d_ids))
    for side, at in ((0, 0), (1, nblk - 2)):
        loads.start(m.at[at : at + 2], m_edge.at[2 * side : 2 * side + 2])
        loads.start(t.at[at : at + 2], t_v.at[at : at + 2])
    loads.start(t.at[near:nblk, :, columns(z[0], zc)], f.at[near:nblk, :, w : w + zc])
    for g, (rows, want, t_id, d_ids) in enumerate(needs):
        at = 0
        for part, m_id in want:
            loads.wait(m_id)
            band_rows(
                part, [b - 2 for b in part], off, c, w, m_v, 0,
                ys.at[at * BK : (at + len(part)) * BK],
            )
            at += len(part)
        loads.wait(t_id)
        project(p_out, None if g == 0 else p_out, ys, t_v, rows[0], len(rows))
        if d_ids:
            loads.wait(*d_ids, whole)
            band_rows(lead, range(len(lead)), off, f, w + zc, d_v, 0, yd)
            project(r_out, None, yd, t_v, lead[0], len(lead))
        if g == 1:
            loads.ahead = 64
            loads.go()
    loads.wait_all()


def first(z, off, c, t, m, d, zc):
    nblk, _, w = c.shape
    nt = t.shape[2]
    inner = nblk - 4
    count = len(lead_of(nblk)[0])
    macs = inner * BK * w * (KB * BK + nt) + count * BK * (w + zc) * (KB * BK + nt)
    return pl.pallas_call(
        functools.partial(first_kernel, nblk),
        out_shape=(
            pltpu.VMEM((w, nt), F32),
            pltpu.VMEM((w + zc, nt), F32),
            pltpu.VMEM((nblk, BK, w + zc), BF16),
            pltpu.VMEM((nblk, BK, nt), BF16),
            pltpu.VMEM((4, KB, BK, BK), BF16),
        ),
        in_specs=[SMEM, SMEM, VMEM, ANY, ANY, ANY],
        out_specs=(VMEM,) * 5,
        scratch_shapes=[
            pltpu.VMEM((inner, KB, BK, BK), BF16),
            pltpu.VMEM((count, KB, BK, BK), BF16),
            pltpu.VMEM((4 * BK, w), BF16),
            pltpu.VMEM((count * BK, w + zc), BF16),
            pltpu.SemaphoreType.DMA((5 * len(groups_of(nblk)) + 9,)),
        ],
        compiler_params=params(15),
        cost_estimate=cost(macs, 30 * 2**20),
    )(z, off, held(c), stay(t), stay(m), stay(d))


def middle_kernel(groups, off, after, acc, f, t, d, d_rest, out, d_edge, yd, sems):
    nblk = f.shape[0]
    loads = Loads(sems)
    for side, at in ((0, 0), (1, nblk - 2)):
        loads.start(d.at[at : at + 2], d_edge.at[2 * side : 2 * side + 2])
    for g, rows in enumerate(groups):
        slot = rows[0] - groups[0][0]
        band_rows(rows, range(slot, slot + len(rows)), off, f, f.shape[2], d_rest, 0, yd)
        project(out, acc if g == 0 else out, yd, t, rows[0], len(rows))
    loads.wait_all()


def middle(off, after, acc, f, t, d, d_rest):
    nblk, _, nt = t.shape
    cols = acc.shape[0]
    groups = lead_of(nblk)[1]
    count = sum(map(len, groups))
    return pl.pallas_call(
        functools.partial(middle_kernel, groups),
        out_shape=(pltpu.VMEM((cols, nt), F32), pltpu.VMEM((4, KB, BK, BK), BF16)),
        in_specs=[SMEM, ANY] + [VMEM] * 3 + [ANY, VMEM],
        out_specs=(VMEM, VMEM),
        scratch_shapes=[
            pltpu.VMEM((MOST * BK, cols), BF16),
            pltpu.SemaphoreType.DMA((2,)),
        ],
        compiler_params=params(6),
        cost_estimate=cost(count * BK * cols * (KB * BK + nt), 14 * 2**20),
    )(off, after, held(acc), held(f), held(t), stay(d), held(d_rest))


def boundary_start(nblk, core, f, intra, inter, f_v, sems):
    loads = Loads(sems)
    low = 10 * (1 - core)
    loads.start(f.at[0:4], f_v.at[2:6])
    loads.start(intra, f_v.at[pl.ds(low, 2)])
    loads.start(inter, f_v.at[pl.ds(10 - low, 2)])
    loads.start(f.at[nblk - 4 : nblk], f_v.at[6:10])
    return loads


def boundary_rows(nblk, loads, off, blocks, f_v, ys, at=0):
    cols = f_v.shape[2]
    if loads:
        loads.wait(0, 1, 2)
    band_rows([0, 1], [0, 1], off, f_v, cols, blocks, 2, ys.at[0 : 2 * BK], at)
    if loads:
        loads.wait(3)
    band_rows(
        [nblk - 2, nblk - 1], [2, 3], off, f_v, cols, blocks, 10 - nblk, ys.at[2 * BK : 4 * BK], at
    )


def boundary_sum(acc, ys, t, here, more=()):
    nblk = t.shape[0]
    ends = ((0,), (0,))
    total = acc[here, :]
    for at, rows in ((0, (0, 1)), (2, (nblk - 2, nblk - 1)), (4, more)):
        if rows:
            size = len(rows) * BK
            block = t[rows[0] : rows[-1] + 1].reshape(size, -1)
            total = total + dot(ys[at * BK : at * BK + size, here], block, ends)
    return total


def boundary_kernel(
    nblk, place, off, acc, c, intra, inter, t, m, d,
    send_0, send_1, keep, d_rest, f_v, ys, sems, d_sems,
):
    core = core_of(place)
    w = c.shape[2]
    near = boundary_start(nblk, core, c, intra.at[:, :, 0:w], inter, f_v, sems)
    loads = Loads(d_sems)
    _, rest, _ = lead_of(nblk)
    loads.start(d.at[rest[0][0] : nblk - 2], d_rest)
    half = keep.shape[0]
    boundary_rows(nblk, near, off, m, f_v, ys)
    here = pl.ds(pl.multiple_of(core * half, half), half)
    there = pl.ds(pl.multiple_of((1 - core) * half, half), half)
    away = boundary_sum(acc, ys, t, there).astype(BF16)
    for q, send in enumerate((send_0, send_1)):
        send[...] = away[q * half // 2 : (q + 1) * half // 2, :]
    keep[...] = boundary_sum(acc, ys, t, here)
    loads.wait_all()


def project_boundary(place, off, acc, c, intra, inter, t, m, d):
    nblk, _, nt = t.shape
    w = acc.shape[0]
    others = nblk - 2 - lead_of(nblk)[1][0][0]
    return pl.pallas_call(
        functools.partial(boundary_kernel, nblk),
        out_shape=(
            *[jax.ShapeDtypeStruct((w // 4, nt), BF16)] * 2,
            jax.ShapeDtypeStruct((w // 2, nt), F32),
            pltpu.VMEM((others, KB, BK, BK), BF16),
            pltpu.VMEM((12, BK, w), BF16),
        ),
        in_specs=[SMEM, SMEM] + [VMEM] * 6 + [ANY],
        out_specs=(VMEM,) * 5,
        scratch_shapes=[
            pltpu.VMEM((4 * BK, w), BF16),
            pltpu.SemaphoreType.DMA((4,)),
            pltpu.SemaphoreType.DMA((1,)),
        ],
        compiler_params=params(10),
        cost_estimate=cost(BK, BK),
    )(place, off, held(acc), held(c), intra, inter, held(t), held(m), stay(d))


def merge_kernel(count, skip, after, a, *refs):
    got, out = refs[:count], refs[count + skip]
    rows = a.shape[0] // count
    for q in range(count):
        here = slice(q * rows, (q + 1) * rows)
        out[here, :] = (a[here, :].astype(F32) + got[q][...].astype(F32)).astype(BF16)


def merge(after, a, got, hold=False, also=()):
    shapes = [jax.ShapeDtypeStruct(a.shape, BF16)]
    if hold:
        shapes.append(jax.ShapeDtypeStruct(after.shape, after.dtype))
    out = pl.pallas_call(
        functools.partial(merge_kernel, len(got), len(also)),
        out_shape=shapes,
        in_specs=[ANY, VMEM] + [VMEM] * len(got) + [ANY] * len(also),
        out_specs=[VMEM, ANY][: len(shapes)],
        input_output_aliases={0: 1} if hold else {},
        compiler_params=params(8),
    )(after, a, *got, *also)
    return out if hold else out[0]


def square_sum(x):
    x = x.astype(F32)
    return jnp.sum(x * x, axis=0, keepdims=True)


def orth_rows(c, t, p):
    return (c.astype(F32) - dot(t, p, ((1,), (1,)))).astype(BF16)


def orth_rows32(c, t, p):
    return c.astype(F32) - dot(t, p, ((1,), (1,)))


def orth_kernel(own, part, place, p, after, x_in, sq_in, c, t, x_out, sq, x_v, out_sems):
    nblk, _, nt = t.shape
    half = p.shape[0]
    core = core_of(place)
    side = core if own else 1 - core
    here = pl.ds(pl.multiple_of(side * half, half), half)
    stores = Loads(out_sems)
    total = None
    for at in range(part[0], part[1], 2):
        block = c[at : at + 2, :, here].reshape(2 * BK, half)
        x = orth_rows32(block, t[at : at + 2].reshape(2 * BK, nt), p[...])
        x_v[at : at + 2] = x.astype(BF16).reshape(2, BK, half)
        squares = square_sum(x)
        total = squares if total is None else total + squares
        stores.start(x_v.at[at : at + 2], x_out.at[at : at + 2, :, here])
    sq[...] = sq_in[...]
    sq[:, here] += total
    stores.wait_all()


def orthogonalize(own, part, place, p, after, x, sq, c, t):
    nblk, _, nt = t.shape
    half = p.shape[0]
    w = 2 * half
    return pl.pallas_call(
        functools.partial(orth_kernel, own, part),
        out_shape=(pltpu.HBM((nblk, BK, w), BF16), jax.ShapeDtypeStruct((1, w), F32)),
        in_specs=[SMEM, VMEM, ANY, ANY, VMEM, VMEM, VMEM],
        out_specs=(ANY, VMEM),
        input_output_aliases={} if x is None else {3: 0},
        scratch_shapes=[
            pltpu.VMEM((nblk, BK, half), BF16),
            pltpu.SemaphoreType.DMA((nblk,)),
        ],
        compiler_params=params(7),
        cost_estimate=cost(nblk * BK * half * nt, 8 * 2**20),
    )(place, p, after, after if x is None else x, sq, held(c), held(t))


def chip_order(bits, side):
    return [(s + side) % bits for s in range(bits)]


def dipole_boundary_kernel(
    nblk, place, off, after, acc, f, near, intra, tz_inter, t, d, d_rest,
    send_0, send_1, keep, f_v, ys, sems,
):
    groups, cols, lanes = keep.shape
    w = near.shape[2]
    bits = groups.bit_length() - 1
    loads = boundary_start(
        nblk, core_of(place), f.at[:, :, w:cols], intra.at[:, :, w:cols], tz_inter, f_v, sems
    )
    _, rest, last = lead_of(nblk)
    slot = last[0] - rest[0][0]
    band_rows(last, range(slot, slot + len(last)), off, f, cols, d_rest, 0, ys.at[4 * BK :])
    boundary_rows(nblk, None, off, d, near, ys)
    boundary_rows(nblk, loads, off, d, f_v, ys, w)
    orders = [chip_order(bits, side) for side in (0, 1)]
    for at in range(0, cols, BK):
        here = slice(at, min(at + BK, cols))
        whole = boundary_sum(acc, ys, t, here, last)
        for g in range(groups):
            owned = []
            for side in (0, 1):
                chip = sum(
                    ((g >> (bits - 1 - s)) & 1) << orders[side][s] for s in range(bits)
                )
                first_lane = (2 * chip + side) * lanes
                owned.append(whole[:, first_lane : first_lane + lanes])
            keep[g, here, :] = jnp.where(core_of(place) == 0, owned[0], owned[1])
            send = (send_0, send_1)[2 * g // groups]
            away = jnp.where(core_of(place) == 0, owned[1], owned[0])
            send[g % (groups // 2), here, :] = away.astype(BF16)


def dipole_boundary(place, off, after, acc, f, near, intra, tz_inter, t, d, d_rest, groups):
    nblk, _, nt = t.shape
    cols = acc.shape[0]
    lanes = nt // (2 * groups)
    return pl.pallas_call(
        functools.partial(dipole_boundary_kernel, nblk),
        out_shape=(
            jax.ShapeDtypeStruct((groups // 2, cols, lanes), BF16),
            jax.ShapeDtypeStruct((groups // 2, cols, lanes), BF16),
            jax.ShapeDtypeStruct((groups, cols, lanes), F32),
        ),
        in_specs=[SMEM, SMEM, ANY] + [VMEM] * 8,
        out_specs=(VMEM,) * 3,
        scratch_shapes=[
            pltpu.VMEM((12, BK, tz_inter.shape[2]), BF16),
            pltpu.VMEM(((4 + LAST) * BK, cols), BF16),
            pltpu.SemaphoreType.DMA((4,)),
        ],
        compiler_params=params(11),
        cost_estimate=cost(4 * BK * cols * (KB * BK + nt), 8 * 2**20),
    )(place, off, after, held(acc), held(f), held(near), intra, tz_inter, held(t), held(d), held(d_rest))


def halve_kernel(step, place, after, keep, *refs):
    got, (send, kept, _) = refs[:-3], refs[-3:]
    half = kept.shape[0]
    orders = [chip_order(step[1], side)[step[0]] for side in (0, 1)]
    which = jnp.where(core_of(place) == 0, orders[0], orders[1])
    bit = jnp.bitwise_and(jnp.right_shift(place[0], which + 1), 1)

    def come(of, g):
        if len(got) == 1:
            return got[0][of * half + g].astype(F32)
        return jnp.where(of == 0, got[0][g], got[1][g]).astype(F32)

    for g in range(half):
        kept[g] = keep[bit * half + g] + come(bit, g)
        send[g] = (keep[(1 - bit) * half + g] + come(1 - bit, g)).astype(BF16)


def halve(step, place, after, keep, got):
    groups, cols, lanes = keep.shape
    half = groups // 2
    return pl.pallas_call(
        functools.partial(halve_kernel, step),
        out_shape=(
            jax.ShapeDtypeStruct((half, cols, lanes), BF16),
            jax.ShapeDtypeStruct((half, cols, lanes), F32),
            jax.ShapeDtypeStruct(after.shape, after.dtype),
        ),
        in_specs=[SMEM, ANY, VMEM] + [VMEM] * len(got),
        out_specs=(VMEM, VMEM, ANY),
        input_output_aliases={1: 2},
        compiler_params=params(8),
    )(place, after, keep, *got)


def settle_kernel(w, after, keep, got, out):
    out[...] = (keep[0, w:, :] + got[0, w:, :].astype(F32)).astype(BF16)


def settle(w, after, keep, got):
    _, cols, lanes = keep.shape
    return pl.pallas_call(
        functools.partial(settle_kernel, w),
        out_shape=jax.ShapeDtypeStruct((cols - w, lanes), BF16),
        in_specs=[ANY, VMEM, VMEM],
        out_specs=VMEM,
        compiler_params=params(8),
    )(after, keep, got)


def stack_kernel(after, *refs):
    out, at = refs[-1], 0
    for piece in refs[:-1]:
        out[at : at + piece.shape[0], :] = piece[...]
        at += piece.shape[0]


def stack(after, pieces):
    rows = sum(piece.shape[0] for piece in pieces)
    return pl.pallas_call(
        stack_kernel,
        out_shape=jax.ShapeDtypeStruct((rows, pieces[0].shape[1]), BF16),
        in_specs=[ANY] + [VMEM] * len(pieces),
        out_specs=VMEM,
        compiler_params=params(8),
    )(after, *pieces)


def finish_kernel(rows, spots, place, z, keep, got, mine, other, sq, *refs):
    pieces, (out, g_v) = refs[:-2], refs[-2:]
    half, w = mine.shape[0], sq.shape[1]
    zc = keep.shape[1] - w
    at = 0
    for piece in pieces:
        for q in range(piece.shape[0] // zc):
            where = pl.multiple_of(jnp.bitwise_xor(z[0], spots[at]) * zc, zc)
            g_v[pl.ds(where, zc), :] = piece[q * zc : (q + 1) * zc, :]
            at += 1
    norm = 1.0 / jnp.sqrt(sq[...] / rows + 1e-06)
    for side in (0, 1):
        here = slice(side * half, (side + 1) * half)
        p = jnp.where(core_of(place) == side, mine[...], other[...])
        raw = keep[0, here, :] + got[0, here, :].astype(F32) - dot(p, g_v[...])
        out[:, here] = (raw.T * norm[:, here]).astype(BF16)


def finish(rows, spots, place, z, keep, got, mine, other, sq, pieces):
    _, cols, lanes = keep.shape
    nt = mine.shape[1]
    w = sq.shape[1]
    return pl.pallas_call(
        functools.partial(finish_kernel, rows, spots),
        out_shape=jax.ShapeDtypeStruct((lanes, w), BF16),
        in_specs=[SMEM, SMEM] + [VMEM] * (5 + len(pieces)),
        out_specs=VMEM,
        scratch_shapes=[pltpu.VMEM((nt, lanes), BF16)],
        compiler_params=params(8),
    )(place, z, keep, got, mine, other, sq, *pieces)


def swap(block, count, mask):
    return lax.ppermute(block, "basis", [(i, i ^ mask[i % 2]) for i in range(count)])


def meet(block, count):
    pairs = [(i, i + 1) for i in range(1, count - 1, 2)]
    return lax.ppermute(block, "basis", pairs + [(b, a) for a, b in pairs])


def exchange(intra, inter, count):
    inter = meet(inter, count)
    return swap(intra, count, (1, 1)), inter


def scalar(x):
    return x.astype(jnp.int32).reshape(1)


def on_device(cont_orbitals, target_orbitals, margin_blocks, dipole_blocks, band_offsets):
    count = lax.axis_size("basis")
    planes = lax.axis_size("orb")
    rows, w = cont_orbitals.shape
    nblk = rows // BK
    nt = target_orbitals.shape[1]
    zc = nt // planes
    chips = count // 2
    bits = chips.bit_length() - 1
    place_s = scalar(lax.axis_index("basis"))
    z = lax.axis_index("orb")
    z_s = scalar(z)
    off = band_offsets.astype(jnp.int32).T
    c = cont_orbitals.reshape(nblk, BK, w)
    t = target_orbitals.reshape(nblk, BK, nt)
    zero = jnp.zeros((1, w), F32)
    both = (1, 1)
    orders = [chip_order(bits, side) for side in (0, 1)]
    masks = [(2 << orders[0][s], 2 << orders[1][s]) for s in range(bits)]

    intra, inter, tz_inter = edges(place_s, z_s, c, t, zc)
    intra, inter = exchange(intra, inter, count)
    tz_inter = meet(tz_inter, count)
    p_acc, r_acc, f, t_v, m_edge = first(z_s, off, c, t, margin_blocks, dipole_blocks, zc)
    *sends, keep, d_rest, near = project_boundary(
        place_s, off, p_acc, c, intra, inter, t_v, m_edge, dipole_blocks
    )
    got = [swap(send, count, both) for send in sends]
    part, r_acc = merge(r_acc, keep, got, hold=True, also=(tz_inter,))

    for s in range(bits):
        got = [swap(part, count, masks[s])]
        if s == 0:
            r_acc, d_edge = middle(off, part, r_acc, f, t_v, dipole_blocks, d_rest)
            part, r_acc = merge(r_acc, part, got, hold=True)
            continue
        if s == 1:
            *sends, keep = dipole_boundary(
                place_s, off, part, r_acc, f, near, intra, tz_inter, t_v, d_edge, d_rest, chips
            )
            got_r = [swap(send, count, both) for send in sends]
            send = sends[0]
        else:
            send, keep, part = halve((s - 2, bits), place_s, part, keep, got_r)
            got_r = [swap(send, count, masks[s - 2])]
        part = merge(send, part, got)
    send, keep, part = halve((bits - 2, bits), place_s, part, keep, got_r)
    got_r = [swap(send, count, masks[bits - 2])]
    other = swap(part, count, both)

    x, sq = orthogonalize(True, (0, nblk), place_s, part, part, None, zero, c, t_v)
    x, sq = orthogonalize(False, (0, nblk), place_s, other, part, x, sq, c, t_v)
    send, keep, sq = halve((bits - 1, bits), place_s, sq, keep, got_r)
    got_r = [swap(send, count, masks[bits - 1])]
    tail = [both] + masks
    sq = sq + swap(sq, count, tail.pop(0))
    sq = sq + swap(sq, count, tail.pop(0))
    pieces = [settle(w, sq, keep, got_r[0])]
    spots, step = [0], planes // 2
    while step:
        whole = pieces[0]
        if len(pieces) > 1:
            whole = stack(sq, pieces)
        pieces.append(lax.ppermute(whole, "orb", [(i, i ^ step) for i in range(planes)]))
        spots += [spot ^ step for spot in spots]
        step //= 2
    for mask in tail:
        sq = sq + swap(sq, count, mask)
    dipole_mo = finish(rows * count, spots, place_s, z_s, keep, got_r[0], part, other, sq, pieces)
    return (x.reshape(rows, w), dipole_mo)


def solution(mesh):
    return jax.shard_map(
        on_device,
        mesh=mesh,
        in_specs=(
            P("basis", "orb"),
            P("basis", None),
            P("basis", None, None, None),
            P("basis", None, None, None),
            P("basis", None),
        ),
        out_specs=(P("basis", "orb"), P("basis", "orb")),
        check_vma=False,
    )
```
